128 devices in a mesh: strip: 4 (over x), tile: 32 (over z, y, core).
Axes of the slice: x: 4, y: 4, z: 4, core: 2. Of those that a mesh axis runs over, the one named last changes fastest.
Arguments:
- right_side: float32 [8, 4, 384, 32, 256], P('strip', None, 'tile'), may hold values from -1.2 to 1.2
- starting_iterate: float32 [8, 4, 384, 32, 256], P('strip', None, 'tile'), may hold values from -1.2 to 1.2
- inverse_diagonal_blocks: bfloat16 [8, 4, 384, 256, 256], P('strip', None, 'tile'), may hold values from -0.15 to 1, as said below
- couple: float32 [6, 8, 4, 384, 256], P(None, 'strip', None, 'tile'), may hold values from 0.02 to 2, as said below
- ice_mask: int32 [8, 4, 384], P('strip', None, 'tile'), may hold values 0 or 1
Outputs:
- solution_field: float32 [8, 4, 384, 32, 256], P('strip', None, 'tile')
The draws below stay inside these ranges and needn't reach their ends.
Inputs may be any that keep to these rules, and one draw needn't show every extreme that they name: `inverse_diagonal_blocks`: each block is an inverse diagonal block of a diagonally dominant operator. `couple`: all couplings are positive.
All inputs are finite; a program needn't handle non-finite values. No bound on the sum of `ice_mask` on one device may be relied on, other than what follows from the above.
Results may differ from the reference program's by a relative error of at most 0.014.
Values sent between devices are 32-bit elements; how exact they have to be, the bound alone decides.
No kernel may reach another device: no remote copies, remote signals or barrier semaphores. Data moves between devices by JAX's collectives and lax.ppermute only.
A program may use at most 128 MiB of HBM per device.

```python
import math
import jax
import jax.numpy as jnp
from jax import lax

BS = 256
R = 32
NC = 4
STRIPS = 8
LANES = 384


def inverse_scale(key):
    return jax.random.uniform(jax.random.fold_in(key, 11), (STRIPS, NC, LANES, BS), jnp.float32, 0.5, 1.0)


def draw_inverse_diagonal_blocks(key, part):
    magnitude_multiplier = inverse_scale(key)
    key = jax.random.fold_in(key, 5)
    shape = (STRIPS, NC, LANES, BS, BS)
    identity = jnp.eye(BS, dtype=jnp.float32)
    spread = 0.2 / math.sqrt(BS)
    offdiag = jnp.clip(spread * jax.random.normal(key, shape, jnp.float32), -4.0 * spread, 4.0 * spread)
    return ((identity + (1.0 - identity) * offdiag) * magnitude_multiplier[..., None, :]).astype(jnp.bfloat16)


def carry_rates(key, slow_share, low_keep, high_keep, magnitude_multiplier):
    key_pick, key_keep, key_fast, key_spot, key_drop = jax.random.split(key, 5)
    chain = STRIPS * NC
    keep = jax.random.uniform(key_keep, (LANES, 1), jnp.float32, low_keep, high_keep)
    slow_rate = jnp.exp(jnp.log(keep) / chain)
    fast_rate = jnp.exp(jax.random.uniform(key_fast, (LANES, BS), jnp.float32, math.log(0.05), math.log(0.4)))
    chosen = jax.random.uniform(key_pick, (LANES, BS), jnp.float32) < slow_share
    falloff_speed = jnp.where(chosen, slow_rate, fast_rate)
    column = jnp.arange(STRIPS)[:, None] * NC + jnp.arange(NC)[None, :]
    spots = jax.random.randint(key_spot, (2, LANES), 0, chain)
    damaged_nodes = (column[:, :, None] == spots[0][None, None, :]) | (column[:, :, None] == spots[1][None, None, :])
    removed_share = jax.random.uniform(key_drop, (STRIPS, NC, LANES), jnp.float32, 0.65, 0.8)
    spike_span = jnp.where(damaged_nodes, removed_share, 1.0)
    return falloff_speed[None, None] * spike_span[..., None] / magnitude_multiplier


def draw_couple(key, part):
    magnitude_multiplier = inverse_scale(key)
    key = jax.random.fold_in(key, 7)
    key_up, key_down, key_side = jax.random.split(key, 3)
    lateral_extent = (4, STRIPS, NC, LANES, BS)
    upstream = carry_rates(key_up, 0.5, 0.35, 0.6, magnitude_multiplier)
    lower_flowward = carry_rates(key_down, 0.5, 0.35, 0.6, magnitude_multiplier)
    side = jnp.exp(jax.random.uniform(key_side, lateral_extent, jnp.float32, math.log(0.02), math.log(0.15)))
    return jnp.concatenate([upstream[None], lower_flowward[None], side], 0)


def touch_ends(result, rng, smallest, largest):
    extent = result.shape
    index_at = [jax.random.randint(jax.random.fold_in(rng, axis), (), 0, extent[axis]) for axis in range(len(extent))]
    result = result.at[tuple(index_at)].set(smallest)
    longest = extent.index(max(extent))
    index_at[longest] = (index_at[longest] + 1) % extent[longest]
    return result.at[tuple(index_at)].set(largest)


def steps_of(stream_key, extent, cuts, least, top_value):
    def one(dim, blocks):
        heights = jax.random.uniform(jax.random.fold_in(jax.random.fold_in(stream_key, 6), dim), (blocks,), jnp.float32, least / len(cuts), top_value / len(cuts))
        return jnp.repeat(jnp.exp(heights), extent[dim] // blocks).reshape((-1,) + (1,) * (len(extent) - dim - 1))

    level = one(*cuts[0])
    for cut in cuts[1:]:
        level = level * one(*cut)
    return level


def scatter_about(key, dims, scale, most, shards=(), kind=jnp.bfloat16):
    entries = jax.random.normal(key, dims, jnp.float32) * scale
    if len(shards) > 0:
        entries = steps_of(key, dims, shards, -0.22, 0.18) * entries
    return jnp.clip(entries, min=-most, max=most).astype(kind)


def setup_inputs(seed: int = 0) -> dict:
    key_of = jax.random.split(jax.random.key(seed), 6)
    right_side = scatter_about(key_of[0], (STRIPS, NC, LANES, R, BS), 0.2, 1.2, ((0, 4), (2, 32)), jnp.float32)
    starting_iterate = scatter_about(key_of[1], (STRIPS, NC, LANES, R, BS), 0.2, 1.2, ((0, 4), (2, 32)), jnp.float32)
    inverse_diagonal_blocks = draw_inverse_diagonal_blocks(jax.random.fold_in(key_of[5], 71), 0)
    couple = draw_couple(jax.random.fold_in(key_of[5], 71), 0)
    ice_mask = touch_ends((jax.random.randint(key_of[4], (STRIPS, NC, LANES), 0, 16) < 15).astype(jnp.int32), jax.random.fold_in(key_of[4], 1), 0, 1)
    return {"right_side": right_side, "starting_iterate": starting_iterate, "inverse_diagonal_blocks": inverse_diagonal_blocks, "couple": couple, "ice_mask": ice_mask}


def lateral(field, couple):
    lane_count = field.shape[2]
    padded = jnp.pad(field, ((0, 0), (0, 0), (2, 2), (0, 0), (0, 0)))
    total = couple[2][:, :, :, None, :] * padded[:, :, 1:lane_count + 1]
    total = total + couple[3][:, :, :, None, :] * padded[:, :, 3:lane_count + 3]
    total = total + couple[4][:, :, :, None, :] * padded[:, :, 0:lane_count]
    total = total + couple[5][:, :, :, None, :] * padded[:, :, 4:lane_count + 4]
    return total


def flatten(array):
    return array.reshape((array.shape[0] * array.shape[1],) + array.shape[2:])


def solve_block(inverse_col, source_col, weight_col):
    rounded = lax.optimization_barrier(source_col.astype(jnp.bfloat16)).astype(jnp.float32)
    solved = jnp.einsum('lij,lrj->lri', inverse_col.astype(jnp.float32), rounded, precision=lax.Precision.HIGHEST)
    return weight_col * solved


def reference(right_side, starting_iterate, inverse_diagonal_blocks, couple, ice_mask):
    ice_weight = ice_mask.astype(jnp.float32)[:, :, :, None, None]
    initial = ice_weight * starting_iterate
    inverse = flatten(inverse_diagonal_blocks)
    weight = flatten(ice_weight)
    up_coef = flatten(couple[0])[:, :, None, :]
    down_coef = flatten(couple[1])[:, :, None, :]
    old = flatten(initial)
    zeroed = jnp.zeros_like(old[0])
    source = flatten(right_side + lateral(initial, couple))
    down_old = jnp.concatenate([old[1:], zeroed[None]], 0)

    def advance_fwd(previous, items):
        source_col, higher_flow_column, down_col, inverse_col, weight_col, lagged_col = items
        solved = solve_block(inverse_col, source_col + higher_flow_column * previous + down_col * lagged_col, weight_col)
        return solved, solved

    last, forward = lax.scan(advance_fwd, zeroed, (source, up_coef, down_coef, inverse, weight, down_old))
    forward_full = forward.reshape(initial.shape)
    source_b = flatten(right_side + lateral(forward_full, couple))
    up_old = jnp.concatenate([zeroed[None], forward[:-1]], 0)

    def advance_bwd(following, items):
        source_col, higher_flow_column, down_col, inverse_col, weight_col, lagged_col = items
        solved = solve_block(inverse_col, source_col + higher_flow_column * lagged_col + down_col * following, weight_col)
        return solved, solved

    first, backward = lax.scan(advance_bwd, zeroed, (source_b, up_coef, down_coef, inverse, weight, up_old), reverse=True)
    return backward.reshape(initial.shape)
```

```python
import functools

import jax
import jax.numpy as jnp
from jax import lax
from jax.experimental import pallas as pl
from jax.experimental.pallas import tpu as pltpu
from jax.sharding import PartitionSpec as P

COLS = 8
LANES = 12
R = 32
BS = 256
CHUNKS = ((2, 3, 4, 5), (6, 7, 8, 9), (0, 1, 10, 11))
EDGE = 2
STRIP = 4
NT = (((1,), (1,)), ((), ()))
VMEM = pltpu.VMEM
ANY = pl.ANY


def runs_of(lanes):
    runs = []
    for lane in lanes:
        if runs and runs[-1][0] + runs[-1][1] == lane:
            runs[-1][1] += 1
        else:
            runs.append([lane, 1])
    return [tuple(run) for run in runs]


def place_of(chunk, lane):
    if chunk == 0:
        return lane
    if chunk == 1:
        return lane - 4
    return lane + 2 if lane < 6 else lane - 2


def solve(xs, inverse, q, lanes):
    return [
        lax.dot_general(
            x.astype(jnp.bfloat16), inverse[q, lane], NT, preferred_element_type=jnp.float32
        )
        for x, lane in zip(xs, lanes)
    ]


def coef(ref, k, q, lane):
    return ref[k, q, pl.ds(lane, 1), :]


def weight(ref, q, lane):
    return ref[q, pl.ds(lane, 1), :]


def forward_chain(lanes, stage_edge, q, source, inverse, couple, mask, field, carry, left, right):
    xs = [source[q, lane] + coef(couple, 0, q, lane) * carry[j] for j, lane in enumerate(lanes)]
    ys = solve(xs, inverse, q, lanes)
    for j, lane in enumerate(lanes):
        value = weight(mask, q, lane) * ys[j]
        field[q + 1, lane] = value
        carry[j] = value
        if stage_edge:
            if lane < 2:
                left[q, lane] = value
            else:
                right[q, lane - (LANES - 2)] = value


def first_kernel(chunk, *refs):
    lanes = CHUNKS[chunk]
    edge = chunk == EDGE
    refs = list(refs)
    inv_hbm, rs_hbm, st_hbm, nxt, couple, mask = refs[:6]
    refs = refs[6:]
    if edge:
        halo_l, halo_r = refs[:2]
        refs = refs[2:]
    if chunk > 0:
        refs = refs[4:]
    inverse, rs, source, field = refs[:4]
    refs = refs[4:]
    if edge:
        left, right = refs[:2]
        refs = refs[2:]
    else:
        left = right = None
    sent, start, carry, sem_inv, sem_rs, sem_st = refs
    active = lax.axis_index("strip") == 0

    if edge:
        st_runs = [(0, 4, 2), (8, 4, 6)]
    else:
        st_runs = [(lanes[0] - 2, 8, 0)]

    def st_copies(q):
        return [
            pltpu.make_async_copy(
                st_hbm.at[q, pl.ds(a, n)], start.at[q, pl.ds(b, n)], sem_st.at[q]
            )
            for a, n, b in st_runs
        ] + (
            [
                pltpu.make_async_copy(halo_l.at[q], start.at[q, pl.ds(0, 2)], sem_st.at[q]),
                pltpu.make_async_copy(halo_r.at[q], start.at[q, pl.ds(10, 2)], sem_st.at[q]),
            ]
            if edge
            else []
        )

    def nxt_copies():
        at, copies = 0, []
        for a, n in runs_of(lanes):
            copies.append(
                pltpu.make_async_copy(
                    nxt.at[pl.ds(at, n)],
                    start.at[COLS, pl.ds(place_of(chunk, a), n)],
                    sem_st.at[COLS],
                )
            )
            at += n
        return copies

    def rs_copies(q):
        return [
            pltpu.make_async_copy(rs_hbm.at[q, pl.ds(a, n)], rs.at[q, pl.ds(a, n)], sem_rs.at[q])
            for a, n in runs_of(lanes)
        ]

    def inv_copies(q):
        return [
            pltpu.make_async_copy(
                inv_hbm.at[q, pl.ds(a, n)], inverse.at[q, pl.ds(a, n)], sem_inv.at[q]
            )
            for a, n in runs_of(lanes)
        ]

    for copy in st_copies(0) + st_copies(1) + rs_copies(0) + inv_copies(0):
        copy.start()

    def launch(q, _):
        for copy in st_copies(q + 1) + rs_copies(q) + inv_copies(q):
            copy.start()
        return 0

    lax.fori_loop(1, COLS - 1, launch, 0)
    for copy in nxt_copies() + rs_copies(COLS - 1) + inv_copies(COLS - 1):
        copy.start()

    def make_source(q):
        for lane in lanes:
            total = rs[q, lane]
            for k, step in ((2, -1), (3, 1), (4, -2), (5, 2)):
                other = lane + step
                factor = coef(couple, k, q, lane)
                if 0 <= other < LANES:
                    factor = factor * weight(mask, q, other)
                total = total + factor * start[q, place_of(chunk, other)]
            factor = coef(couple, 1, q, lane) * weight(mask, q + 1, lane)
            source[q, lane] = total + factor * start[q + 1, place_of(chunk, lane)]

    def wait_source(q):
        for copy in rs_copies(q):
            copy.wait()

        @pl.when(q < COLS - 1)
        def _():
            for copy in st_copies(q + 1):
                copy.wait()

        @pl.when(q == COLS - 1)
        def _():
            for copy in nxt_copies():
                copy.wait()

    for copy in st_copies(0):
        copy.wait()

    @pl.when(active)
    def _():
        for lane in lanes:
            field[0, lane] = jnp.zeros((R, BS), jnp.float32)
        carry[...] = jnp.zeros_like(carry)
        wait_source(0)
        make_source(0)

        def step(q, _):
            later = jnp.minimum(q + 1, COLS - 1)

            @pl.when(q < COLS - 1)
            def _():
                wait_source(later)

            for copy in inv_copies(q):
                copy.wait()
            forward_chain(
                lanes, edge, q, source, inverse, couple, mask, field, carry, left, right
            )
            make_source(later)
            return 0

        lax.fori_loop(0, COLS, step, 0)
        sent[...] = carry[...]

    @pl.when(jnp.logical_not(active))
    def _():
        def step(q, _):
            wait_source(q)
            make_source(q)
            return 0

        lax.fori_loop(0, COLS, step, 0)

        def drain(q, _):
            for copy in inv_copies(q):
                copy.wait()
            return 0

        lax.fori_loop(0, COLS, drain, 0)


def forward_kernel(chunk, stage, *refs):
    lanes = CHUNKS[chunk]
    edge = chunk == EDGE
    refs = list(refs)
    came, inverse, source, couple, mask = refs[:5]
    refs = refs[5:]
    if edge:
        _, _, _, field, left, right, sent = refs[:7]
        refs = refs[7:]
    else:
        _, field, sent = refs[:3]
        refs = refs[3:]
        left = right = None
    (carry,) = refs
    active = lax.axis_index("strip") == stage

    @pl.when(active)
    def _():
        for j, lane in enumerate(lanes):
            carry[j] = came[j]
            field[0, lane] = came[j]

        def step(q, _):
            forward_chain(
                lanes, edge, q, source, inverse, couple, mask, field, carry, left, right
            )
            return 0

        lax.fori_loop(0, COLS, step, 0)
        sent[...] = carry[...]


def backward_chain(lanes, q, source, inverse, couple, mask, carry, result):
    xs = [source[q, lane] + coef(couple, 1, q, lane) * carry[j] for j, lane in enumerate(lanes)]
    ys = solve(xs, inverse, q, lanes)
    for j, lane in enumerate(lanes):
        value = weight(mask, q, lane) * ys[j]
        result[q, j] = value
        carry[j] = value


def result_copies(lanes, q, result, out, sem):
    at, copies = 0, []
    for a, n in runs_of(lanes):
        copies.append(
            pltpu.make_async_copy(
                result.at[q, pl.ds(at, n)], out.at[q, pl.ds(a, n)], sem.at[q]
            )
        )
        at += n
    return copies


def last_kernel(chunk, *refs):
    lanes = CHUNKS[chunk]
    edge = chunk == EDGE
    refs = list(refs)
    inverse, rs, field, couple, mask = refs[:5]
    refs = refs[5:]
    if edge:
        halo_l, halo_r = refs[:2]
        refs = refs[2:]
    refs = refs[1:]
    if chunk > 0:
        refs = refs[1:]
    source, out, sent, carry, result, sem = refs
    active = lax.axis_index("strip") == STRIP - 1

    def near(q, lane):
        if lane < 0:
            return halo_l[q, lane + 2]
        if lane >= LANES:
            return halo_r[q, lane - LANES]
        return field[q + 1, lane]

    def make_source(q):
        for lane in lanes:
            total = rs[q, lane] + coef(couple, 0, q, lane) * field[q, lane]
            for k, step in ((2, -1), (3, 1), (4, -2), (5, 2)):
                total = total + coef(couple, k, q, lane) * near(q, lane + step)
            source[q, lane] = total

    @pl.when(active)
    def _():
        carry[...] = jnp.zeros_like(carry)
        make_source(COLS - 1)

        def step(i, _):
            q = COLS - 1 - i
            backward_chain(lanes, q, source, inverse, couple, mask, carry, result)
            for copy in result_copies(lanes, q, result, out, sem):
                copy.start()
            make_source(jnp.maximum(q - 1, 0))
            return 0

        lax.fori_loop(0, COLS, step, 0)
        sent[...] = carry[...]

        def drain(q, _):
            for copy in result_copies(lanes, q, result, out, sem):
                copy.wait()
            return 0

        lax.fori_loop(0, COLS, drain, 0)

    @pl.when(jnp.logical_not(active))
    def _():
        def step(q, _):
            make_source(q)
            return 0

        lax.fori_loop(0, COLS, step, 0)


def backward_kernel(chunk, stage, came, inverse, source, couple, mask, _, out, sent, carry, result, sem):
    lanes = CHUNKS[chunk]
    active = lax.axis_index("strip") == stage

    @pl.when(active)
    def _():
        carry[...] = came[...]

        def step(i, _):
            q = COLS - 1 - i
            backward_chain(lanes, q, source, inverse, couple, mask, carry, result)
            for copy in result_copies(lanes, q, result, out, sem):
                copy.start()
            return 0

        lax.fori_loop(0, COLS, step, 0)
        sent[...] = carry[...]

        def drain(q, _):
            for copy in result_copies(lanes, q, result, out, sem):
                copy.wait()
            return 0

        lax.fori_loop(0, COLS, drain, 0)


def vmem(shape, dtype=jnp.float32):
    return VMEM(shape, dtype)


def held(array):
    return pltpu.with_memory_space_constraint(array, VMEM)


def run(kernel, name, operands, outs, scratch, aliases):
    arrays = [held(a) if space is VMEM else a for a, space in operands]
    return pl.pallas_call(
        kernel,
        name=name,
        out_shape=[o for o, _ in outs],
        in_specs=[pl.BlockSpec(memory_space=space) for _, space in operands],
        out_specs=[pl.BlockSpec(memory_space=space) for _, space in outs],
        scratch_shapes=scratch,
        input_output_aliases=aliases,
        compiler_params=pltpu.CompilerParams(vmem_limit_bytes=16 * 2**20),
        cost_estimate=pl.CostEstimate(flops=2**27, bytes_accessed=2**22, transcendentals=0),
    )(*arrays)


FIELD = (COLS, LANES, R, BS)
FIELD_IN = (COLS + 1, LANES, R, BS)
PIECE = (4, R, BS)
SIDE = (COLS, 2, R, BS)


def on_device(right_side, starting_iterate, inverse_diagonal_blocks, couple, ice_mask):
    rs_hbm = right_side.reshape(FIELD)
    st_hbm = starting_iterate.reshape(FIELD)
    inv_hbm = inverse_diagonal_blocks.reshape((COLS, LANES, BS, BS))
    coefs = couple.reshape((6, COLS, LANES, BS))
    flat_mask = ice_mask.reshape((COLS, LANES)).astype(jnp.float32)
    mask = jnp.broadcast_to(
        jnp.concatenate([flat_mask, jnp.ones((1, LANES), jnp.float32)], 0)[:, :, None],
        (COLS + 1, LANES, BS),
    )
    weights = flat_mask[:, :, None, None]
    tiles = lax.axis_size("tile")
    to_right = [(i, i + 1) for i in range(tiles - 1)]
    to_left = [(i + 1, i) for i in range(tiles - 1)]
    to_back = [(i + 1, i) for i in range(STRIP - 1)]

    nxt = []
    for lanes in CHUNKS:
        first = jnp.concatenate(
            [weights[0, a : a + n] * st_hbm[0, a : a + n] for a, n in runs_of(lanes)], 0
        )
        nxt.append(lax.ppermute(first, "strip", to_back))
    start_l = lax.ppermute(weights[:, LANES - 2 :] * st_hbm[:, LANES - 2 :], "tile", to_right)
    start_r = lax.ppermute(weights[:, :2] * st_hbm[:, :2], "tile", to_left)

    dma = pltpu.SemaphoreType.DMA
    piece = vmem(PIECE)
    inverse = rs = source = field = left = right = None
    sents = []
    for chunk in range(3):
        operands = [
            (inv_hbm, ANY), (rs_hbm, ANY), (st_hbm, ANY), (nxt[chunk], ANY), (coefs, VMEM), (mask, VMEM),
        ]
        outs = [
            (vmem((COLS, LANES, BS, BS), jnp.bfloat16), VMEM),
            (vmem(FIELD), VMEM),
            (vmem(FIELD), VMEM),
            (vmem(FIELD_IN), VMEM),
        ]
        if chunk == EDGE:
            operands += [(start_l, ANY), (start_r, ANY)]
            outs += [(vmem(SIDE), VMEM), (vmem(SIDE), VMEM)]
        outs.append((vmem(PIECE), VMEM))
        aliases = {}
        if chunk > 0:
            base = len(operands)
            operands += [(inverse, VMEM), (rs, VMEM), (source, VMEM), (field, VMEM)]
            aliases = {base + i: i for i in range(4)}
        got = run(
            functools.partial(first_kernel, chunk),
            f"first_{chunk}",
            operands,
            outs,
            [
                vmem((COLS + 1, 12, R, BS)),
                piece,
                dma((COLS,)),
                dma((COLS,)),
                dma((COLS + 1,)),
            ],
            aliases,
        )
        inverse, rs, source, field = got[:4]
        if chunk == EDGE:
            left, right = got[4:6]
        sents.append(got[-1])

    for stage in range(1, STRIP):
        cames = [lax.ppermute(sent, "strip", [(stage - 1, stage)]) for sent in sents]
        sents = []
        for chunk in range(3):
            operands = [(cames[chunk], VMEM), (inverse, VMEM), (source, VMEM), (coefs, VMEM), (mask, VMEM)]
            outs = [(vmem(FIELD_IN), VMEM)]
            base = len(operands)
            operands += [(field, VMEM)]
            aliases = {base: 0}
            if chunk == EDGE:
                operands += [(left, VMEM), (right, VMEM)]
                outs += [(vmem(SIDE), VMEM), (vmem(SIDE), VMEM)]
                aliases |= {base + 1: 1, base + 2: 2}
            outs.append((vmem(PIECE), VMEM))
            got = run(
                functools.partial(forward_kernel, chunk, stage),
                f"forward_{stage}_{chunk}",
                operands,
                outs,
                [piece],
                aliases,
            )
            field = got[0]
            if chunk == EDGE:
                left, right = got[1:3]
            sents.append(got[-1])

    halo_l = lax.ppermute(right, "tile", to_right)
    halo_r = lax.ppermute(left, "tile", to_left)

    out_shape = jax.ShapeDtypeStruct(FIELD, jnp.float32)
    out_scratch = [piece, vmem((COLS,) + PIECE), dma((COLS,))]
    out = None
    sents = []
    for chunk in range(3):
        operands = [(inverse, VMEM), (rs, VMEM), (field, VMEM), (coefs, VMEM), (mask, VMEM)]
        if chunk == EDGE:
            operands += [(halo_l, VMEM), (halo_r, VMEM)]
        base = len(operands)
        operands += [(source, VMEM)]
        aliases = {base: 0}
        if chunk > 0:
            operands += [(out, ANY)]
            aliases[base + 1] = 1
        source, out, sent = run(
            functools.partial(last_kernel, chunk),
            f"last_{chunk}",
            operands,
            [(vmem(FIELD), VMEM), (out_shape, ANY), (vmem(PIECE), VMEM)],
            out_scratch,
            aliases,
        )
        sents.append(sent)

    for stage in range(STRIP - 2, -1, -1):
        cames = [lax.ppermute(sent, "strip", [(stage + 1, stage)]) for sent in sents]
        sents = []
        for chunk in range(3):
            operands = [
                (cames[chunk], VMEM), (inverse, VMEM), (source, VMEM), (coefs, VMEM), (mask, VMEM), (out, ANY),
            ]
            out, sent = run(
                functools.partial(backward_kernel, chunk, stage),
                f"backward_{stage}_{chunk}",
                operands,
                [(out_shape, ANY), (vmem(PIECE), VMEM)],
                out_scratch,
                {5: 0},
            )
            sents.append(sent)
    return out.reshape(right_side.shape)


def solution(mesh):
    return jax.shard_map(
        on_device,
        mesh=mesh,
        in_specs=(
            P("strip", None, "tile", None, None),
            P("strip", None, "tile", None, None),
            P("strip", None, "tile", None, None),
            P(None, "strip", None, "tile", None),
            P("strip", None, "tile"),
        ),
        out_specs=P("strip", None, "tile", None, None),
        check_vma=False,
    )
```

```python
import functools

import jax
import jax.numpy as jnp
from jax import lax
from jax.experimental import pallas as pl
from jax.experimental.pallas import tpu as pltpu
from jax.sharding import PartitionSpec as P

COLS = 8
LANES = 12
R = 32
BS = 256
FORWARD = ((2, 3, 4, 5), (6, 7, 8, 9), (0, 1, 10, 11))
BACKWARD = ((2, 3, 4, 5), (6, 7, 8, 9), (0, 1, 10, 11))
STRIP = 4
SIDES = ((2, -1), (3, 1), (4, -2), (5, 2))
NT = (((1,), (1,)), ((), ()))
VMEM = pltpu.VMEM
ANY = pl.ANY
HBM = pltpu.HBM

FIELD = (COLS, LANES, R, BS)
FIELD_MORE = (COLS + 1, LANES, R, BS)
EDGE = (COLS, 2, R, BS)
BLOCKS = (COLS, LANES, BS, BS)
PER = 4
COEFS = (6, COLS // PER, LANES, PER, BS)
WEIGHTS = (COLS + 1, LANES, BS)


def runs_of(lanes):
    runs = []
    for lane in lanes:
        if runs and runs[-1][0] + runs[-1][1] == lane:
            runs[-1][1] += 1
        else:
            runs.append([lane, 1])
    return [tuple(run) for run in runs]


def coef(ref, k, q, lane):
    return ref[k, q // PER, lane, pl.ds(q % PER, 1), :]


def weight(ref, q, lane):
    return ref[q, pl.ds(lane, 1), :]


def solve(xs, inverse, q, lanes):
    return [
        lax.dot_general(
            x.astype(jnp.bfloat16), inverse[q, lane], NT, preferred_element_type=jnp.float32
        )
        for x, lane in zip(xs, lanes)
    ]


def lane_copies(src, dst, q, lanes, sem):
    return [
        pltpu.make_async_copy(src.at[q, pl.ds(a, n)], dst.at[q, pl.ds(a, n)], sem.at[q])
        for a, n in runs_of(lanes)
    ]


def prep_kernel(ice, st_hbm, couple_hbm, first, edge_l, edge_r, couple, mask, sem):
    copies = [
        pltpu.make_async_copy(st_hbm.at[0], first, sem.at[0]),
        pltpu.make_async_copy(st_hbm.at[:, pl.ds(0, 2)], edge_l, sem.at[1]),
        pltpu.make_async_copy(st_hbm.at[:, pl.ds(LANES - 2, 2)], edge_r, sem.at[2]),
        pltpu.make_async_copy(couple_hbm, couple, sem.at[3]),
    ]
    for copy in copies:
        copy.start()

    def ice_weight(q, lane):
        return ice[q // PER, q % PER, lane].astype(jnp.float32)

    for q in range(COLS):
        for lane in range(LANES):
            mask[q, pl.ds(lane, 1), :] = jnp.full((1, BS), ice_weight(q, lane), jnp.float32)
    mask[COLS] = jnp.ones((LANES, BS), jnp.float32)
    copies[0].wait()
    for lane in range(LANES):
        first[lane] = weight(mask, 0, lane) * first[lane]
    copies[1].wait()
    copies[2].wait()

    def scale(q, _):
        for j in range(2):
            edge_l[q, j] = weight(mask, q, j) * edge_l[q, j]
            edge_r[q, j] = weight(mask, q, LANES - 2 + j) * edge_r[q, j]
        return 0

    lax.fori_loop(0, COLS, scale, 0)
    copies[3].wait()


def make_source(lanes, q, rs, start, couple, mask, source, halo_l=None, halo_r=None):
    for lane in lanes:
        total = rs[q, lane]
        for k, step in SIDES:
            other = lane + step
            if 0 <= other < LANES:
                factor = coef(couple, k, q, lane) * weight(mask, q, other)
                total = total + factor * start[q, other]
            elif other < 0 and halo_l is not None:
                total = total + coef(couple, k, q, lane) * halo_l[q, other + 2]
            elif other >= LANES and halo_r is not None:
                total = total + coef(couple, k, q, lane) * halo_r[q, other - LANES]
        factor = coef(couple, 1, q, lane) * weight(mask, q + 1, lane)
        source[q, lane] = total + factor * start[q + 1, lane]


def forward_chain(lanes, q, source, inverse, couple, mask, field, sent, left=None, right=None):
    xs = [source[q, lane] + coef(couple, 0, q, lane) * sent[j] for j, lane in enumerate(lanes)]
    ys = solve(xs, inverse, q, lanes)
    for j, lane in enumerate(lanes):
        value = weight(mask, q, lane) * ys[j]
        field[q + 1, lane] = value
        sent[j] = value
        if left is not None and lane < 2:
            left[q, lane] = value
        if right is not None and lane >= LANES - 2:
            right[q, lane - (LANES - 2)] = value


def first_kernel(
    inv_hbm, rs_hbm, st_hbm, couple, mask, inverse, rs, start, source, field, sent, sem_a, sem_b, sem_st
):
    lanes, later_lanes = FORWARD[0], FORWARD[1]

    def column(q):
        return lane_copies(inv_hbm, inverse, q, lanes, sem_a) + lane_copies(
            rs_hbm, rs, q, lanes, sem_a
        )

    def column_later(q):
        return lane_copies(inv_hbm, inverse, q, later_lanes, sem_b) + lane_copies(
            rs_hbm, rs, q, later_lanes, sem_b
        )

    def column_start(q):
        return lane_copies(st_hbm, start, q, range(LANES), sem_st)

    def launch(q, _):
        for copy in column(q):
            copy.start()

        @pl.when(q < COLS - 1)
        def _():
            for copy in column_start(q + 1):
                copy.start()

        return 0

    def launch_later(q, _):
        for copy in column_later(q):
            copy.start()
        return 0

    def wait_for(copies):
        for copy in copies:
            copy.wait()

    @pl.when(lax.axis_index("strip") == 0)
    def _():
        for copy in column_start(0):
            copy.start()
        lax.fori_loop(0, COLS, launch, 0)
        lax.fori_loop(0, COLS, launch_later, 0)
        for j, lane in enumerate(lanes):
            sent[j] = jnp.zeros((R, BS), jnp.float32)
        field[0] = jnp.zeros((LANES, R, BS), jnp.float32)
        wait_for(column_start(0) + column_start(1) + column(0))
        make_source(lanes, 0, rs, start, couple, mask, source)

        def step(q, _):
            later = jnp.minimum(q + 1, COLS - 2)

            @pl.when(q < COLS - 2)
            def _():
                wait_for(column_start(later + 1) + column(later))

            forward_chain(lanes, q, source, inverse, couple, mask, field, sent)
            make_source(lanes, later, rs, start, couple, mask, source)
            return 0

        lax.fori_loop(0, COLS - 1, step, 0)
        wait_for(column(COLS - 1))

        def drain(q, _):
            wait_for(column_later(q))
            return 0

        lax.fori_loop(0, COLS, drain, 0)


def tail_kernel(nxt, rs, couple, mask, inverse, *refs):
    start, source, field, sent = refs[4:]
    lanes = FORWARD[0]
    start[COLS] = nxt[...]

    @pl.when(lax.axis_index("strip") == 0)
    def _():
        make_source(lanes, COLS - 1, rs, start, couple, mask, source)
        forward_chain(lanes, COLS - 1, source, inverse, couple, mask, field, sent)


def load_kernel(inv_hbm, rs_hbm, st_hbm, couple, mask, *refs):
    inverse, rs, start, source, field, sent, sem_inv, sem_rs, sem_st = refs[5:]
    first = lax.axis_index("strip") == 0
    lanes, last_lanes = FORWARD[1], FORWARD[2]
    every = range(LANES)

    def wait_for(copies):
        for copy in copies:
            copy.wait()

    @pl.when(first)
    def _():
        def column(q):
            return lane_copies(inv_hbm, inverse, q, last_lanes, sem_inv) + lane_copies(
                rs_hbm, rs, q, last_lanes, sem_rs
            )

        def launch(q, _):
            for copy in column(q):
                copy.start()
            return 0

        lax.fori_loop(0, COLS, launch, 0)
        for j, lane in enumerate(lanes):
            sent[j] = jnp.zeros((R, BS), jnp.float32)
        make_source(lanes, 0, rs, start, couple, mask, source)

        def step(q, _):
            forward_chain(lanes, q, source, inverse, couple, mask, field, sent)
            make_source(
                lanes, jnp.minimum(q + 1, COLS - 1), rs, start, couple, mask, source
            )
            return 0

        lax.fori_loop(0, COLS, step, 0)

        def drain(q, _):
            wait_for(column(q))
            return 0

        lax.fori_loop(0, COLS, drain, 0)

    @pl.when(jnp.logical_not(first))
    def _():
        def launch(q, _):
            for copy in (
                lane_copies(st_hbm, start, q, every, sem_st)
                + lane_copies(rs_hbm, rs, q, every, sem_rs)
                + lane_copies(inv_hbm, inverse, q, every, sem_inv)
            ):
                copy.start()
            return 0

        lax.fori_loop(0, COLS, launch, 0)
        wait_for(lane_copies(st_hbm, start, 0, every, sem_st))

        def step(q, _):
            wait_for(lane_copies(rs_hbm, rs, q, every, sem_rs))

            @pl.when(q < COLS - 1)
            def _():
                wait_for(lane_copies(st_hbm, start, q + 1, every, sem_st))

            make_source(every, q, rs, start, couple, mask, source)
            return 0

        lax.fori_loop(0, COLS, step, 0)

        def drain(q, _):
            wait_for(lane_copies(inv_hbm, inverse, q, every, sem_inv))
            return 0

        lax.fori_loop(0, COLS, drain, 0)


def edge_kernel(halo_l, halo_r, inverse, rs, start, couple, mask, *refs):
    source, field, left, right, sent = refs[2:]
    lanes = FORWARD[2]
    first = lax.axis_index("strip") == 0

    @pl.when(first)
    def _():
        for j in range(len(lanes)):
            sent[j] = jnp.zeros((R, BS), jnp.float32)

        def source_of(q):
            make_source(lanes, q, rs, start, couple, mask, source, halo_l, halo_r)

        source_of(0)

        def step(q, _):
            forward_chain(lanes, q, source, inverse, couple, mask, field, sent, left, right)
            source_of(jnp.minimum(q + 1, COLS - 1))
            return 0

        lax.fori_loop(0, COLS, step, 0)

    @pl.when(jnp.logical_not(first))
    def _():
        def step(q, _):
            for lane in lanes:
                total = source[q, lane]
                for k, move in SIDES:
                    other = lane + move
                    if other < 0:
                        total = total + coef(couple, k, q, lane) * halo_l[q, other + 2]
                    elif other >= LANES:
                        total = total + coef(couple, k, q, lane) * halo_r[q, other - LANES]
                source[q, lane] = total
            return 0

        lax.fori_loop(0, COLS, step, 0)


def forward_kernel(chunk, stage, came, inverse, source, couple, mask, *refs):
    lanes = FORWARD[chunk]
    left = right = None
    if chunk == 2:
        field, left, right, sent = refs[3:]
    else:
        field, sent = refs[1:]

    @pl.when(lax.axis_index("strip") == stage)
    def _():
        for j, lane in enumerate(lanes):
            sent[j] = came[j]
            field[0, lane] = came[j]

        def step(q, _):
            forward_chain(lanes, q, source, inverse, couple, mask, field, sent, left, right)
            return 0

        lax.fori_loop(0, COLS, step, 0)


def backward_chain(lanes, q, source, inverse, couple, mask, result, sent):
    xs = [source[q, lane] + coef(couple, 1, q, lane) * sent[j] for j, lane in enumerate(lanes)]
    ys = solve(xs, inverse, q, lanes)
    for j, lane in enumerate(lanes):
        value = weight(mask, q, lane) * ys[j]
        result[q, lane] = value
        sent[j] = value


def backward_sweep(chunk, inverse, source, couple, mask, result, out, sent, sem, sem_own, beside):
    lanes = BACKWARD[chunk]
    last = chunk == len(BACKWARD) - 1

    def before(q):
        return lane_copies(result, out, q, BACKWARD[chunk - 1], sem) if chunk > 0 else []

    def own(q):
        return lane_copies(result, out, q, lanes, sem_own) if last else []

    def launch(q, _):
        for copy in before(q):
            copy.start()
        return 0

    lax.fori_loop(0, COLS, launch, 0)

    def step(i, _):
        q = COLS - 1 - i
        backward_chain(lanes, q, source, inverse, couple, mask, result, sent)
        for copy in own(q):
            copy.start()
        if beside is not None:
            beside(jnp.maximum(q - 1, 0))
        return 0

    lax.fori_loop(0, COLS, step, 0)

    def drain(q, _):
        for copy in before(q) + own(q):
            copy.wait()
        return 0

    lax.fori_loop(0, COLS, drain, 0)


def last_kernel(chunk, inverse, rs, field, couple, mask, halo_l, halo_r, *refs):
    lanes = BACKWARD[chunk]
    source, result, out, sent, sem, sem_own = refs[-6:]
    active = lax.axis_index("strip") == STRIP - 1

    def near(q, lane):
        if lane < 0:
            return halo_l[q, lane + 2]
        if lane >= LANES:
            return halo_r[q, lane - LANES]
        return field[q + 1, lane]

    def source_of(q):
        for lane in lanes:
            total = rs[q, lane] + coef(couple, 0, q, lane) * field[q, lane]
            for k, step in SIDES:
                total = total + coef(couple, k, q, lane) * near(q, lane + step)
            source[q, lane] = total

    @pl.when(active)
    def _():
        for j in range(len(lanes)):
            sent[j] = jnp.zeros((R, BS), jnp.float32)
        source_of(COLS - 1)
        backward_sweep(
            chunk, inverse, source, couple, mask, result, out, sent, sem, sem_own, source_of
        )

    @pl.when(jnp.logical_not(active))
    def _():
        def step(q, _):
            source_of(q)
            return 0

        lax.fori_loop(0, COLS, step, 0)


def backward_kernel(chunk, stage, came, inverse, source, couple, mask, *refs):
    result, out, sent, sem, sem_own = refs[2:]

    @pl.when(lax.axis_index("strip") == stage)
    def _():
        sent[...] = came[...]
        backward_sweep(
            chunk, inverse, source, couple, mask, result, out, sent, sem, sem_own, None
        )


def vmem(shape, dtype=jnp.float32):
    return VMEM(shape, dtype)


def run(kernel, name, operands, outs, scratch, aliases=None):
    arrays = [
        pltpu.with_memory_space_constraint(a, space) if space in (VMEM, HBM) else a
        for a, space in operands
    ]
    return pl.pallas_call(
        kernel,
        name=name,
        out_shape=[o for o, _ in outs],
        in_specs=[pl.BlockSpec(memory_space=space) for _, space in operands],
        out_specs=[pl.BlockSpec(memory_space=space) for _, space in outs],
        scratch_shapes=scratch,
        input_output_aliases=aliases or {},
        compiler_params=pltpu.CompilerParams(vmem_limit_bytes=8 * 2**20),
        cost_estimate=pl.CostEstimate(flops=2**26, bytes_accessed=2**21, transcendentals=0),
    )(*arrays)


def on_device(right_side, starting_iterate, inverse_diagonal_blocks, couple, ice_mask):
    rs_hbm = right_side.reshape(FIELD)
    st_hbm = starting_iterate.reshape(FIELD)
    inv_hbm = inverse_diagonal_blocks.reshape(BLOCKS)
    tiles = lax.axis_size("tile")
    to_right = [(i, i + 1) for i in range(tiles - 1)]
    to_left = [(i + 1, i) for i in range(tiles - 1)]
    to_back = [(i + 1, i) for i in range(STRIP - 1)]
    dma = pltpu.SemaphoreType.DMA

    def inside(*arrays):
        return [(a, VMEM) for a in arrays]

    def made(*shapes):
        return [(vmem(shape), VMEM) for shape in shapes]

    def piece(lanes):
        return (len(lanes), R, BS)

    first, edge_l, edge_r, coefs, mask = run(
        prep_kernel,
        "prep",
        [(ice_mask, pltpu.SMEM), (st_hbm, HBM), (couple.transpose(0, 1, 3, 2, 4), HBM)],
        made((LANES, R, BS), EDGE, EDGE, COEFS, WEIGHTS),
        [dma((4,))],
    )
    nxt = lax.ppermute(first, "strip", to_back)
    start_l = lax.ppermute(edge_r, "tile", to_right)
    start_r = lax.ppermute(edge_l, "tile", to_left)

    inverse, rs, start, source, field, sent = run(
        first_kernel,
        "first",
        [(inv_hbm, HBM), (rs_hbm, HBM), (st_hbm, HBM)] + inside(coefs, mask),
        [(vmem(BLOCKS, jnp.bfloat16), VMEM)]
        + made(FIELD, FIELD_MORE, FIELD, FIELD_MORE, piece(FORWARD[0])),
        [dma((COLS,)), dma((COLS,)), dma((COLS,))],
    )
    start, source, field, sent = run(
        tail_kernel,
        "tail",
        inside(nxt, rs, coefs, mask, inverse, start, source, field, sent),
        made(FIELD_MORE, FIELD, FIELD_MORE, piece(FORWARD[0])),
        [],
        {5: 0, 6: 1, 7: 2, 8: 3},
    )
    sents = {(0, 0): sent}
    inverse, rs, start, source, field, sents[0, 1] = run(
        load_kernel,
        "load",
        [(inv_hbm, HBM), (rs_hbm, HBM), (st_hbm, HBM)]
        + inside(coefs, mask, inverse, rs, start, source, field),
        [(vmem(BLOCKS, jnp.bfloat16), VMEM)]
        + made(FIELD, FIELD_MORE, FIELD, FIELD_MORE, piece(FORWARD[1])),
        [dma((COLS,)), dma((COLS,)), dma((COLS,))],
        {5: 0, 6: 1, 7: 2, 8: 3, 9: 4},
    )
    source, field, left, right, sents[0, 2] = run(
        edge_kernel,
        "edge",
        inside(start_l, start_r, inverse, rs, start, coefs, mask, source, field),
        made(FIELD, FIELD_MORE, EDGE, EDGE, piece(FORWARD[2])),
        [],
        {7: 0, 8: 1},
    )

    for stage in range(1, STRIP):
        for chunk, lanes in enumerate(FORWARD):
            came = lax.ppermute(sents[stage - 1, chunk], "strip", [(stage - 1, stage)])
            sending = stage + 1 < STRIP
            operands = inside(came, inverse, source, coefs, mask, field)
            outs = made(FIELD_MORE)
            aliases = {5: 0}
            if chunk == 2:
                operands += inside(left, right)
                outs += made(EDGE, EDGE)
                aliases |= {6: 1, 7: 2}
            got = run(
                functools.partial(forward_kernel, chunk, stage),
                f"forward_{stage}_{chunk}",
                operands,
                outs + (made(piece(lanes)) if sending else []),
                [] if sending else [vmem(piece(lanes))],
                aliases,
            )
            field = got[0]
            if chunk == 2:
                left, right = got[1:3]
            if sending:
                sents[stage, chunk] = got[-1]

    halo_l = lax.ppermute(right, "tile", to_right)
    halo_r = lax.ppermute(left, "tile", to_left)

    out_shape = [(jax.ShapeDtypeStruct(FIELD, jnp.float32), HBM)]
    sems = [dma((COLS,)), dma((COLS,))]
    result = out = None
    for chunk, lanes in enumerate(BACKWARD):
        sides = inside(halo_l, halo_r) if min(lanes) < 2 or max(lanes) >= LANES - 2 else []
        operands = inside(inverse, rs, field, coefs, mask) + sides + inside(source)
        base = len(operands) - 1
        aliases = {base: 0}
        kernel = functools.partial(last_kernel, chunk)
        if not sides:
            kernel = functools.partial(without_halos, kernel)
        if chunk > 0:
            operands += inside(result) + [(out, HBM)]
            aliases |= {base + 1: 1, base + 2: 2}
        source, result, out, sents[STRIP - 1, chunk] = run(
            kernel,
            f"last_{chunk}",
            operands,
            made(FIELD, FIELD) + out_shape + made(piece(lanes)),
            sems,
            aliases,
        )

    for stage in range(STRIP - 2, -1, -1):
        for chunk, lanes in enumerate(BACKWARD):
            came = lax.ppermute(sents[stage + 1, chunk], "strip", [(stage + 1, stage)])
            sending = stage > 0
            got = run(
                functools.partial(backward_kernel, chunk, stage),
                f"backward_{stage}_{chunk}",
                inside(came, inverse, source, coefs, mask, result) + [(out, HBM)],
                made(FIELD) + out_shape + (made(piece(lanes)) if sending else []),
                ([] if sending else [vmem(piece(lanes))]) + sems,
                {5: 0, 6: 1},
            )
            result, out = got[:2]
            if sending:
                sents[stage, chunk] = got[2]
    return out.reshape(right_side.shape)


def without_halos(kernel, inverse, rs, field, couple, mask, *refs):
    kernel(inverse, rs, field, couple, mask, None, None, *refs)


def solution(mesh):
    return jax.shard_map(
        on_device,
        mesh=mesh,
        in_specs=(
            P("strip", None, "tile", None, None),
            P("strip", None, "tile", None, None),
            P("strip", None, "tile", None, None),
            P(None, "strip", None, "tile", None),
            P("strip", None, "tile"),
        ),
        out_specs=P("strip", None, "tile", None, None),
        check_vma=False,
    )
```

```python
import functools

import jax
import jax.numpy as jnp
from jax import lax
from jax.experimental import pallas as pl
from jax.experimental.pallas import tpu as pltpu
from jax.sharding import PartitionSpec as P

COLS = 8
LANES = 12
R = 32
BS = 256
FORWARD = ((2, 3, 4, 5), (6, 7, 8, 9), (0, 1, 10, 11))
BACKWARD = ((2, 3, 4, 5), (6, 7, 8, 9), (0, 1, 10, 11))
OUTER = 2
STRIP = 4
SIDES = ((2, -1), (3, 1), (4, -2), (5, 2))
NT = (((1,), (1,)), ((), ()))
VMEM = pltpu.VMEM
ANY = pl.ANY
HBM = pltpu.HBM

FIELD = (COLS, LANES, R, BS)
LATER = (LANES - 4, R, BS)
FIELD_MORE = (COLS + 1, LANES, R, BS)
EDGE = (COLS, 2, R, BS)
BLOCKS = (COLS, LANES, BS, BS)
PER = 4
COEFS = (6, COLS // PER, LANES, PER, BS)
WEIGHTS = (COLS + 1, LANES, BS)


def runs_of(lanes):
    runs = []
    for lane in lanes:
        if runs and runs[-1][0] + runs[-1][1] == lane:
            runs[-1][1] += 1
        else:
            runs.append([lane, 1])
    return [tuple(run) for run in runs]


def coef(ref, k, q, lane):
    return ref[k, q // PER, lane, pl.ds(q % PER, 1), :]


def weight(ref, q, lane):
    return ref[q, pl.ds(lane, 1), :]


def solve(xs, inverse, q, lanes):
    return [
        lax.dot_general(
            x.astype(jnp.bfloat16), inverse[q, lane], NT, preferred_element_type=jnp.float32
        )
        for x, lane in zip(xs, lanes)
    ]


def lane_copies(src, dst, q, lanes, sem):
    return [
        pltpu.make_async_copy(src.at[q, pl.ds(a, n)], dst.at[q, pl.ds(a, n)], sem.at[q])
        for a, n in runs_of(lanes)
    ]


def is_even():
    return lax.axis_index("tile") % 2 == 0


def ice_copy(ice_hbm, ice, sem):
    return pltpu.make_async_copy(ice_hbm, ice, sem)


def ice_weight(ice, q, lane):
    return ice[q // PER, q % PER, lane].astype(jnp.float32)


def near_prep_kernel(ice_hbm, st_hbm, now, later, ice, sem):
    at = 0
    copies = [ice_copy(ice_hbm, ice, sem.at[0])]
    for lanes in FORWARD:
        for a, n in runs_of(lanes):
            if lanes == FORWARD[0]:
                target = now.at[pl.ds(0, n)]
            else:
                target = later.at[pl.ds(at, n)]
                at += n
            copies.append(
                pltpu.make_async_copy(st_hbm.at[0, pl.ds(a, n)], target, sem.at[len(copies)])
            )
    for copy in copies:
        copy.start()
    for copy in copies:
        copy.wait()
    for j, lane in enumerate(FORWARD[0]):
        now[j] = ice_weight(ice, 0, lane) * now[j]
    for j, lane in enumerate(FORWARD[1] + FORWARD[2]):
        later[j] = ice_weight(ice, 0, lane) * later[j]


def prep_kernel(_, ice_hbm, st_hbm, couple_hbm, edge_in, edge_out, couple, mask, ice, sem):
    even = is_even()
    lane_in = jnp.where(even, LANES - 2, 0)
    lane_out = jnp.where(even, 0, LANES - 2)
    copies = [
        ice_copy(ice_hbm, ice, sem.at[0]),
        pltpu.make_async_copy(st_hbm.at[:, pl.ds(lane_out, 2)], edge_out, sem.at[1]),
        pltpu.make_async_copy(st_hbm.at[:, pl.ds(lane_in, 2)], edge_in, sem.at[2]),
        pltpu.make_async_copy(couple_hbm, couple, sem.at[3]),
    ]
    for copy in copies:
        copy.start()
    copies[0].wait()
    for q in range(COLS):
        for lane in range(LANES):
            mask[q, pl.ds(lane, 1), :] = jnp.full((1, BS), ice_weight(ice, q, lane), jnp.float32)
    copies[1].wait()
    copies[2].wait()
    for q in range(COLS):
        for j in range(2):
            edge_out[q, j] = ice_weight(ice, q, lane_out + j) * edge_out[q, j]
            edge_in[q, j] = ice_weight(ice, q, lane_in + j) * edge_in[q, j]
    copies[3].wait()


def halo_of(even, halo_in, halo_out, q, lane):
    if lane < 0:
        return jnp.where(even, halo_out[q, lane + 2], halo_in[q, lane + 2])
    return jnp.where(even, halo_in[q, lane - LANES], halo_out[q, lane - LANES])


def make_source(lanes, q, rs, start, couple, mask, source, halo=None, later=None):
    for j, lane in enumerate(lanes):
        total = rs[q, lane]
        for k, step in SIDES:
            other = lane + step
            if 0 <= other < LANES:
                factor = coef(couple, k, q, lane) * weight(mask, q, other)
                total = total + factor * start[q, other]
            elif halo is not None:
                total = total + coef(couple, k, q, lane) * halo(q, other)
        if later is None:
            factor = coef(couple, 1, q, lane) * weight(mask, q + 1, lane)
            total = total + factor * start[q + 1, lane]
        else:
            total = total + coef(couple, 1, q, lane) * later[j]
        source[q, lane] = total


def forward_chain(lanes, q, source, inverse, couple, mask, field, sent, edges=None):
    xs = [source[q, lane] + coef(couple, 0, q, lane) * sent[j] for j, lane in enumerate(lanes)]
    ys = solve(xs, inverse, q, lanes)
    values = [weight(mask, q, lane) * y for y, lane in zip(ys, lanes)]
    for j, lane in enumerate(lanes):
        field[q + 1, lane] = values[j]
        sent[j] = values[j]
    if edges is not None:
        even, edge_in, edge_out = edges
        for j in range(2):
            edge_in[q, j] = jnp.where(even, values[2 + j], values[j])
            edge_out[q, j] = jnp.where(even, values[j], values[2 + j])


def start_all(copies):
    def step(q, _):
        for copy in copies(q):
            copy.start()
        return 0

    lax.fori_loop(0, COLS, step, 0)


def wait_all(copies):
    def step(q, _):
        for copy in copies(q):
            copy.wait()
        return 0

    lax.fori_loop(0, COLS, step, 0)


def sweep_first(
    lanes, rs, start, source, inverse, couple, mask, field, sent, columns, halo, edges, arriving=None
):
    for j in range(len(lanes)):
        sent[j] = jnp.zeros((R, BS), jnp.float32)
    make_source(lanes, 0, rs, start, couple, mask, source, halo)

    def step(q, _):
        if arriving is not None:
            for copy in arriving(q):
                copy.wait()
        forward_chain(lanes, q, source, inverse, couple, mask, field, sent, edges)
        make_source(
            lanes, jnp.minimum(q + 1, columns - 1), rs, start, couple, mask, source, halo
        )
        return 0

    lax.fori_loop(0, columns, step, 0)


def first_kernel(inv_hbm, rs, start, couple, mask, inverse, source, field, sent, sem, sem_next):
    first = lax.axis_index("strip") == 0

    @pl.when(first)
    def _():
        def own(q):
            return lane_copies(inv_hbm, inverse, q, FORWARD[0], sem)

        def following(q):
            return lane_copies(inv_hbm, inverse, q, FORWARD[1], sem_next)

        start_all(own)
        start_all(following)
        field[0] = jnp.zeros((LANES, R, BS), jnp.float32)
        sweep_first(
            FORWARD[0],
            rs,
            start,
            source,
            inverse,
            couple,
            mask,
            field,
            sent,
            COLS - 1,
            None,
            None,
            own,
        )
        for copy in own(COLS - 1):
            copy.wait()
        wait_all(following)

    @pl.when(jnp.logical_not(first))
    def _():
        def every(q):
            return lane_copies(inv_hbm, inverse, q, range(LANES), sem)

        start_all(every)

        def step(q, _):
            make_source(range(LANES), q, rs, start, couple, mask, source)
            return 0

        lax.fori_loop(0, COLS - 1, step, 0)
        wait_all(every)


def tail_kernel(now, inverse, rs, start, couple, mask, *refs):
    source, field, sent = refs[3:]
    lanes, q = FORWARD[0], COLS - 1

    @pl.when(lax.axis_index("strip") == 0)
    def _():
        make_source(lanes, q, rs, start, couple, mask, source, None, now)
        forward_chain(lanes, q, source, inverse, couple, mask, field, sent)


def outer_kernel(now, later, halo_in, halo_out, inverse, rs, start, couple, mask, *refs):
    source, field, edge_in, edge_out, sent = refs[2:]
    lanes, q_last = FORWARD[OUTER], COLS - 1
    first = lax.axis_index("strip") == 0
    even = is_even()
    edges = (even, edge_in, edge_out)
    halo = functools.partial(halo_of, even, halo_in, halo_out)

    @pl.when(first)
    def _():
        own = later.at[pl.ds(len(FORWARD[1]), len(lanes))]
        sweep_first(
            lanes, rs, start, source, inverse, couple, mask, field, sent, COLS - 1, halo, edges
        )
        make_source(lanes, q_last, rs, start, couple, mask, source, halo, own)
        forward_chain(lanes, q_last, source, inverse, couple, mask, field, sent, edges)

    @pl.when(jnp.logical_not(first))
    def _():
        make_source(FORWARD[0], q_last, rs, start, couple, mask, source, None, now)
        make_source(
            FORWARD[1] + FORWARD[2], q_last, rs, start, couple, mask, source, None, later
        )

        def step(q, _):
            for lane in lanes:
                total = source[q, lane]
                for k, move in SIDES:
                    if not 0 <= lane + move < LANES:
                        total = total + coef(couple, k, q, lane) * halo(q, lane + move)
                source[q, lane] = total
            return 0

        lax.fori_loop(0, COLS, step, 0)


def inner_kernel(later, inv_hbm, rs, start, couple, mask, *refs):
    inverse, source, field, sent, sem = refs[3:]
    lanes, q = FORWARD[1], COLS - 1

    @pl.when(lax.axis_index("strip") == 0)
    def _():
        def following(q):
            return lane_copies(inv_hbm, inverse, q, FORWARD[2], sem)

        start_all(following)
        sweep_first(
            lanes, rs, start, source, inverse, couple, mask, field, sent, COLS - 1, None, None
        )
        make_source(lanes, q, rs, start, couple, mask, source, None, later)
        forward_chain(lanes, q, source, inverse, couple, mask, field, sent)
        wait_all(following)


def forward_kernel(chunk, stage, came, inverse, source, couple, mask, *refs):
    lanes = FORWARD[chunk]
    edges = None
    if chunk == OUTER:
        field, edge_in, edge_out, sent = refs[3:]
        edges = (is_even(), edge_in, edge_out)
    else:
        field, sent = refs[1:]

    @pl.when(lax.axis_index("strip") == stage)
    def _():
        for j, lane in enumerate(lanes):
            sent[j] = came[j]
            field[0, lane] = came[j]

        def step(q, _):
            forward_chain(lanes, q, source, inverse, couple, mask, field, sent, edges)
            return 0

        lax.fori_loop(0, COLS, step, 0)


def backward_chain(lanes, q, source, inverse, couple, mask, result, sent):
    xs = [source[q, lane] + coef(couple, 1, q, lane) * sent[j] for j, lane in enumerate(lanes)]
    ys = solve(xs, inverse, q, lanes)
    for j, lane in enumerate(lanes):
        value = weight(mask, q, lane) * ys[j]
        result[q, lane] = value
        sent[j] = value


def backward_sweep(
    chunk, final, inverse, source, couple, mask, result, out, sent, sem, sem_own, beside
):
    lanes = BACKWARD[chunk]
    last = final and chunk == len(BACKWARD) - 1

    def before(q):
        return lane_copies(result, out, q, BACKWARD[chunk - 1], sem) if chunk > 0 else []

    def own(q):
        return lane_copies(result, out, q, lanes, sem_own) if last else []

    def launch(q, _):
        for copy in before(q):
            copy.start()
        return 0

    lax.fori_loop(0, COLS, launch, 0)

    def step(i, _):
        q = COLS - 1 - i
        backward_chain(lanes, q, source, inverse, couple, mask, result, sent)
        for copy in own(q):
            copy.start()
        if beside is not None:
            beside(jnp.maximum(q - 1, 0))
        return 0

    lax.fori_loop(0, COLS, step, 0)

    def drain(q, _):
        for copy in before(q) + own(q):
            copy.wait()
        return 0

    lax.fori_loop(0, COLS, drain, 0)


def last_kernel(chunk, inverse, rs, field, couple, mask, halo_in, halo_out, *refs):
    lanes = BACKWARD[chunk]
    source, result, out, sent, sem, sem_own = refs[-6:]
    active = lax.axis_index("strip") == STRIP - 1
    even = is_even()

    def near(q, lane):
        if 0 <= lane < LANES:
            return field[q + 1, lane]
        return halo_of(even, halo_in, halo_out, q, lane)

    def source_of(q):
        for lane in lanes:
            total = rs[q, lane] + coef(couple, 0, q, lane) * field[q, lane]
            for k, step in SIDES:
                total = total + coef(couple, k, q, lane) * near(q, lane + step)
            source[q, lane] = total

    @pl.when(active)
    def _():
        for j in range(len(lanes)):
            sent[j] = jnp.zeros((R, BS), jnp.float32)
        source_of(COLS - 1)
        backward_sweep(
            chunk, False, inverse, source, couple, mask, result, out, sent, sem, sem_own, source_of
        )

    @pl.when(jnp.logical_not(active))
    def _():
        def step(q, _):
            source_of(q)
            return 0

        lax.fori_loop(0, COLS, step, 0)


def backward_kernel(chunk, stage, came, inverse, source, couple, mask, *refs):
    result, out, sent, sem, sem_own = refs[2:]
    strip = lax.axis_index("strip")

    @pl.when(strip == stage)
    def _():
        sent[...] = came[...]
        backward_sweep(
            chunk, stage == 0, inverse, source, couple, mask, result, out, sent, sem, sem_own, None
        )

    if chunk == 0:

        @pl.when(strip == stage + 1)
        def _():
            copies = [
                pltpu.make_async_copy(
                    result.at[:, pl.ds(a, n)], out.at[:, pl.ds(a, n)], sem_own.at[i]
                )
                for i, (a, n) in enumerate(runs_of(BACKWARD[-1]))
            ]
            for copy in copies:
                copy.start()
            for copy in copies:
                copy.wait()


def vmem(shape, dtype=jnp.float32):
    return VMEM(shape, dtype)


def run(kernel, name, operands, outs, scratch, aliases=None):
    arrays = [
        pltpu.with_memory_space_constraint(a, space) if space in (VMEM, HBM) else a
        for a, space in operands
    ]
    return pl.pallas_call(
        kernel,
        name=name,
        out_shape=[o for o, _ in outs],
        in_specs=[pl.BlockSpec(memory_space=space) for _, space in operands],
        out_specs=[pl.BlockSpec(memory_space=space) for _, space in outs],
        scratch_shapes=scratch,
        input_output_aliases=aliases or {},
        compiler_params=pltpu.CompilerParams(vmem_limit_bytes=8 * 2**20),
        cost_estimate=pl.CostEstimate(
            flops=2**26, bytes_accessed=2**21, transcendentals=0
        ),
    )(*arrays)


def on_device(right_side, starting_iterate, inverse_diagonal_blocks, couple, ice_mask):
    rs = right_side.reshape(FIELD)
    start = starting_iterate.reshape(FIELD)
    inverse = inverse_diagonal_blocks.reshape(BLOCKS)
    tiles = lax.axis_size("tile")
    pairs_in = [(i, i + 1) for i in range(0, tiles - 1, 2)]
    pairs_out = [(i, i + 1) for i in range(1, tiles - 1, 2)]
    to_back = [(i + 1, i) for i in range(STRIP - 1)]
    dma = pltpu.SemaphoreType.DMA

    def swapped(value, pairs):
        return lax.ppermute(value, "tile", pairs + [(b, a) for a, b in pairs])

    def inside(*arrays):
        return [(a, VMEM) for a in arrays]

    def made(*shapes):
        return [(vmem(shape), VMEM) for shape in shapes]

    def piece(lanes):
        return (len(lanes), R, BS)

    ice = pltpu.SMEM(ice_mask.shape, jnp.int32)
    now, later = run(
        near_prep_kernel,
        "near_prep",
        [(ice_mask, HBM), (start, HBM)],
        made(piece(FORWARD[0]), LATER),
        [ice, dma((6,))],
    )
    now_sent = now
    now = lax.ppermute(now, "strip", to_back)
    edge_in, edge_out, coefs, mask = run(
        prep_kernel,
        "prep",
        inside(now_sent)
        + [(ice_mask, HBM), (start, HBM), (couple.transpose(0, 1, 3, 2, 4), HBM)],
        made(EDGE, EDGE, COEFS, WEIGHTS),
        [ice, dma((4,))],
    )
    halo_out = swapped(edge_out, pairs_out)
    halo_in = swapped(edge_in, pairs_in)
    later = lax.ppermute(later, "strip", to_back)

    sents = {}
    blocks = [(vmem(BLOCKS, jnp.bfloat16), VMEM)]
    inv_hbm = [(inverse, HBM)]
    rest = inside(rs, start, coefs, mask)
    inverse, source, field, sent = run(
        first_kernel,
        "first",
        inv_hbm + rest,
        blocks + made(FIELD, FIELD_MORE, piece(FORWARD[0])),
        [dma((COLS,)), dma((COLS,))],
    )
    source, field, sents[0, 0] = run(
        tail_kernel,
        "tail",
        inside(now, inverse) + rest + inside(source, field, sent),
        made(FIELD, FIELD_MORE, piece(FORWARD[0])),
        [],
        {6: 0, 7: 1, 8: 2},
    )
    inverse, source, field, sents[0, 1] = run(
        inner_kernel,
        "inner",
        inside(later) + inv_hbm + rest + inside(inverse, source, field),
        blocks + made(FIELD, FIELD_MORE, piece(FORWARD[1])),
        [dma((COLS,))],
        {6: 0, 7: 1, 8: 2},
    )
    source, field, edge_in, edge_out, sents[0, 2] = run(
        outer_kernel,
        "outer",
        inside(now, later, halo_in, halo_out, inverse) + rest + inside(source, field),
        made(FIELD, FIELD_MORE, EDGE, EDGE, piece(FORWARD[2])),
        [],
        {9: 0, 10: 1},
    )

    for stage in range(1, STRIP):
        for chunk, lanes in enumerate(FORWARD):
            came = lax.ppermute(sents[stage - 1, chunk], "strip", [(stage - 1, stage)])
            sending = stage + 1 < STRIP
            operands = inside(came, inverse, source, coefs, mask, field)
            outs = made(FIELD_MORE)
            aliases = {5: 0}
            if chunk == OUTER:
                operands += inside(edge_in, edge_out)
                outs += made(EDGE, EDGE)
                aliases |= {6: 1, 7: 2}
            got = run(
                functools.partial(forward_kernel, chunk, stage),
                f"forward_{stage}_{chunk}",
                operands,
                outs + (made(piece(lanes)) if sending else []),
                [] if sending else [vmem(piece(lanes))],
                aliases,
            )
            field = got[0]
            if chunk == OUTER:
                edge_in, edge_out = got[1:3]
            if sending:
                sents[stage, chunk] = got[-1]

    halo_out = swapped(edge_out, pairs_out)
    halo_in = swapped(edge_in, pairs_in)

    out_shape = [(jax.ShapeDtypeStruct(FIELD, jnp.float32), HBM)]
    sems = [dma((COLS,)), dma((COLS,))]
    result = out = None
    for chunk, lanes in enumerate(BACKWARD):
        sides = inside(halo_in, halo_out) if min(lanes) < 2 or max(lanes) >= LANES - 2 else []
        operands = inside(inverse, rs, field, coefs, mask) + sides + inside(source)
        base = len(operands) - 1
        aliases = {base: 0}
        kernel = functools.partial(last_kernel, chunk)
        if not sides:
            kernel = functools.partial(without_halos, kernel)
        if chunk > 0:
            operands += inside(result) + [(out, HBM)]
            aliases |= {base + 1: 1, base + 2: 2}
        source, result, out, sents[STRIP - 1, chunk] = run(
            kernel,
            f"last_{chunk}",
            operands,
            made(FIELD, FIELD) + out_shape + made(piece(lanes)),
            sems,
            aliases,
        )

    for stage in range(STRIP - 2, -1, -1):
        for chunk, lanes in enumerate(BACKWARD):
            came = lax.ppermute(sents[stage + 1, chunk], "strip", [(stage + 1, stage)])
            sending = stage > 0
            got = run(
                functools.partial(backward_kernel, chunk, stage),
                f"backward_{stage}_{chunk}",
                inside(came, inverse, source, coefs, mask, result) + [(out, HBM)],
                made(FIELD) + out_shape + (made(piece(lanes)) if sending else []),
                ([] if sending else [vmem(piece(lanes))]) + sems,
                {5: 0, 6: 1},
            )
            result, out = got[:2]
            if sending:
                sents[stage, chunk] = got[2]
    return out.reshape(right_side.shape)


def without_halos(kernel, inverse, rs, field, couple, mask, *refs):
    kernel(inverse, rs, field, couple, mask, None, None, *refs)


def solution(mesh):
    return jax.shard_map(
        on_device,
        mesh=mesh,
        in_specs=(
            P("strip", None, "tile", None, None),
            P("strip", None, "tile", None, None),
            P("strip", None, "tile", None, None),
            P(None, "strip", None, "tile", None),
            P("strip", None, "tile"),
        ),
        out_specs=P("strip", None, "tile", None, None),
        check_vma=False,
    )
```

```python
import functools

import jax
import jax.numpy as jnp
from jax import lax
from jax.experimental import pallas as pl
from jax.experimental.pallas import tpu as pltpu
from jax.sharding import PartitionSpec as P

COLS = 8
LANES = 12
R = 32
BS = 256
FORWARD = ((2, 3, 4, 5), (6, 7, 8, 9), (0, 1, 10, 11))
BACKWARD = ((2, 3, 4, 5), (6, 7, 8, 9), (0, 1, 10, 11))
OUTER = 2
STRIP = 4
SIDES = ((2, -1), (3, 1), (4, -2), (5, 2))
NT = (((1,), (1,)), ((), ()))
VMEM = pltpu.VMEM
ANY = pl.ANY
HBM = pltpu.HBM

FIELD = (COLS, LANES, R, BS)
LATER = (LANES - 4, R, BS)
FIELD_MORE = (COLS + 1, LANES, R, BS)
EDGE = (COLS, 2, R, BS)
BLOCKS = (COLS, LANES, BS, BS)
PER = 4
COEFS = (6, COLS // PER, LANES, PER, BS)
WEIGHTS = (COLS + 1, LANES, BS)


def runs_of(lanes):
    runs = []
    for lane in lanes:
        if runs and runs[-1][0] + runs[-1][1] == lane:
            runs[-1][1] += 1
        else:
            runs.append([lane, 1])
    return [tuple(run) for run in runs]


def coef(ref, k, q, lane):
    return ref[k, q // PER, lane, pl.ds(q % PER, 1), :]


def weight(ref, q, lane):
    return ref[q, pl.ds(lane, 1), :]


def solve(xs, inverse, q, lanes):
    return [
        lax.dot_general(
            x.astype(jnp.bfloat16), inverse[q, lane], NT, preferred_element_type=jnp.float32
        )
        for x, lane in zip(xs, lanes)
    ]


def lane_copies(src, dst, q, lanes, sem):
    return [
        pltpu.make_async_copy(src.at[q, pl.ds(a, n)], dst.at[q, pl.ds(a, n)], sem.at[q])
        for a, n in runs_of(lanes)
    ]


def is_even():
    return lax.axis_index("tile") % 2 == 0


def ice_copy(ice_hbm, ice, sem):
    return pltpu.make_async_copy(ice_hbm, ice, sem)


def ice_weight(ice, q, lane):
    return ice[q // PER, q % PER, lane].astype(jnp.float32)


def prep_kernel(
    ice_hbm, st_hbm, couple_hbm, inv_hbm, now, later, edge_in, edge_out, couple, mask, inverse, ice, sem, sem_inv
):
    even = is_even()
    lane_in = jnp.where(even, LANES - 2, 0)
    lane_out = jnp.where(even, 0, LANES - 2)
    copies = [
        pltpu.make_async_copy(ice_hbm, ice, sem.at[0]),
        pltpu.make_async_copy(couple_hbm, couple, sem.at[1]),
        pltpu.make_async_copy(st_hbm.at[:, pl.ds(lane_out, 2)], edge_out, sem.at[2]),
        pltpu.make_async_copy(st_hbm.at[:, pl.ds(lane_in, 2)], edge_in, sem.at[3]),
    ]
    at = 0
    for lanes in FORWARD:
        for a, n in runs_of(lanes):
            if lanes == FORWARD[0]:
                target = now.at[pl.ds(0, n)]
            else:
                target = later.at[pl.ds(at, n)]
                at += n
            copies.append(
                pltpu.make_async_copy(st_hbm.at[0, pl.ds(a, n)], target, sem.at[len(copies)])
            )

    def own(q):
        return lane_copies(inv_hbm, inverse, q, FORWARD[0], sem_inv)

    for copy in copies:
        copy.start()
    start_all(own)

    def ice_weight(q, lane):
        return ice[q // PER, q % PER, lane].astype(jnp.float32)

    copies[0].wait()
    for q in range(COLS):
        for lane in range(LANES):
            mask[q, pl.ds(lane, 1), :] = jnp.full((1, BS), ice_weight(q, lane), jnp.float32)
    for copy in copies[1:]:
        copy.wait()
    for q in range(COLS):
        for j in range(2):
            edge_out[q, j] = ice_weight(q, lane_out + j) * edge_out[q, j]
            edge_in[q, j] = ice_weight(q, lane_in + j) * edge_in[q, j]
    for j, lane in enumerate(FORWARD[0]):
        now[j] = weight(mask, 0, lane) * now[j]
    for j, lane in enumerate(FORWARD[1] + FORWARD[2]):
        later[j] = weight(mask, 0, lane) * later[j]
    wait_all(own)


def halo_of(even, halo_in, halo_out, q, lane):
    if lane < 0:
        return jnp.where(even, halo_out[q, lane + 2], halo_in[q, lane + 2])
    return jnp.where(even, halo_in[q, lane - LANES], halo_out[q, lane - LANES])


def make_source(lanes, q, rs, start, couple, mask, source, halo=None, later=None):
    for j, lane in enumerate(lanes):
        total = rs[q, lane]
        for k, step in SIDES:
            other = lane + step
            if 0 <= other < LANES:
                factor = coef(couple, k, q, lane) * weight(mask, q, other)
                total = total + factor * start[q, other]
            elif halo is not None:
                total = total + coef(couple, k, q, lane) * halo(q, other)
        if later is None:
            factor = coef(couple, 1, q, lane) * weight(mask, q + 1, lane)
            total = total + factor * start[q + 1, lane]
        else:
            total = total + coef(couple, 1, q, lane) * later[j]
        source[q, lane] = total


def forward_chain(lanes, q, source, inverse, couple, mask, field, sent, edges=None):
    xs = [source[q, lane] + coef(couple, 0, q, lane) * sent[j] for j, lane in enumerate(lanes)]
    ys = solve(xs, inverse, q, lanes)
    values = [weight(mask, q, lane) * y for y, lane in zip(ys, lanes)]
    for j, lane in enumerate(lanes):
        field[q + 1, lane] = values[j]
        sent[j] = values[j]
    if edges is not None:
        even, edge_in, edge_out = edges
        for j in range(2):
            edge_in[q, j] = jnp.where(even, values[2 + j], values[j])
            edge_out[q, j] = jnp.where(even, values[j], values[2 + j])


def start_all(copies):
    def step(q, _):
        for copy in copies(q):
            copy.start()
        return 0

    lax.fori_loop(0, COLS, step, 0)


def wait_all(copies):
    def step(q, _):
        for copy in copies(q):
            copy.wait()
        return 0

    lax.fori_loop(0, COLS, step, 0)


def sweep_first(
    lanes, rs, start, source, inverse, couple, mask, field, sent, columns, halo, edges
):
    for j in range(len(lanes)):
        sent[j] = jnp.zeros((R, BS), jnp.float32)
    make_source(lanes, 0, rs, start, couple, mask, source, halo)

    def step(q, _):
        forward_chain(lanes, q, source, inverse, couple, mask, field, sent, edges)
        make_source(
            lanes, jnp.minimum(q + 1, columns - 1), rs, start, couple, mask, source, halo
        )
        return 0

    lax.fori_loop(0, columns, step, 0)


def first_kernel(inv_hbm, rs, start, couple, mask, _, inverse, source, field, sent, sem):
    @pl.when(lax.axis_index("strip") == 0)
    def _():
        def following(q):
            return lane_copies(inv_hbm, inverse, q, FORWARD[1], sem)

        start_all(following)
        field[0] = jnp.zeros((LANES, R, BS), jnp.float32)
        sweep_first(
            FORWARD[0], rs, start, source, inverse, couple, mask, field, sent, COLS - 1, None, None
        )
        wait_all(following)


def tail_kernel(now, inverse, rs, start, couple, mask, *refs):
    source, field, sent = refs[3:]
    lanes, q = FORWARD[0], COLS - 1

    @pl.when(lax.axis_index("strip") == 0)
    def _():
        make_source(lanes, q, rs, start, couple, mask, source, None, now)
        forward_chain(lanes, q, source, inverse, couple, mask, field, sent)


def outer_kernel(now, later, halo_in, halo_out, inverse, rs, start, couple, mask, *refs):
    source, field, edge_in, edge_out, sent = refs[2:]
    lanes, q_last = FORWARD[OUTER], COLS - 1
    first = lax.axis_index("strip") == 0
    even = is_even()
    edges = (even, edge_in, edge_out)
    halo = functools.partial(halo_of, even, halo_in, halo_out)

    @pl.when(first)
    def _():
        own = later.at[pl.ds(len(FORWARD[1]), len(lanes))]
        sweep_first(
            lanes, rs, start, source, inverse, couple, mask, field, sent, COLS - 1, halo, edges
        )
        make_source(lanes, q_last, rs, start, couple, mask, source, halo, own)
        forward_chain(lanes, q_last, source, inverse, couple, mask, field, sent, edges)

    @pl.when(jnp.logical_not(first))
    def _():
        make_source(FORWARD[0], q_last, rs, start, couple, mask, source, None, now)
        make_source(
            FORWARD[1] + FORWARD[2], q_last, rs, start, couple, mask, source, None, later
        )

        def step(q, _):
            for lane in lanes:
                total = source[q, lane]
                for k, move in SIDES:
                    if not 0 <= lane + move < LANES:
                        total = total + coef(couple, k, q, lane) * halo(q, lane + move)
                source[q, lane] = total
            return 0

        lax.fori_loop(0, COLS, step, 0)


def inner_kernel(later, inv_hbm, rs, start, couple, mask, *refs):
    inverse, source, field, sent, sem, sem_next = refs[3:]
    lanes, q_last = FORWARD[1], COLS - 1
    first = lax.axis_index("strip") == 0

    def following(q):
        return lane_copies(inv_hbm, inverse, q, FORWARD[2], sem)

    def own(q):
        return lane_copies(inv_hbm, inverse, q, lanes, sem_next)

    @pl.when(first)
    def _():
        start_all(following)
        sweep_first(
            lanes, rs, start, source, inverse, couple, mask, field, sent, COLS - 1, None, None
        )
        make_source(lanes, q_last, rs, start, couple, mask, source, None, later)
        forward_chain(lanes, q_last, source, inverse, couple, mask, field, sent)
        wait_all(following)

    @pl.when(jnp.logical_not(first))
    def _():
        start_all(own)
        start_all(following)

        def step(q, _):
            make_source(range(LANES), q, rs, start, couple, mask, source)
            return 0

        lax.fori_loop(0, COLS - 1, step, 0)
        wait_all(own)
        wait_all(following)


def forward_kernel(chunk, stage, came, inverse, source, couple, mask, *refs):
    lanes = FORWARD[chunk]
    edges = None
    if chunk == OUTER:
        field, edge_in, edge_out, sent = refs[3:]
        edges = (is_even(), edge_in, edge_out)
    else:
        field, sent = refs[1:]

    @pl.when(lax.axis_index("strip") == stage)
    def _():
        for j, lane in enumerate(lanes):
            sent[j] = came[j]
            field[0, lane] = came[j]

        def step(q, _):
            forward_chain(lanes, q, source, inverse, couple, mask, field, sent, edges)
            return 0

        lax.fori_loop(0, COLS, step, 0)


def backward_chain(lanes, q, source, inverse, couple, mask, result, sent):
    xs = [source[q, lane] + coef(couple, 1, q, lane) * sent[j] for j, lane in enumerate(lanes)]
    ys = solve(xs, inverse, q, lanes)
    for j, lane in enumerate(lanes):
        value = weight(mask, q, lane) * ys[j]
        result[q, lane] = value
        sent[j] = value


def backward_sweep(
    chunk, final, inverse, source, couple, mask, result, out, sent, sem, sem_own, beside
):
    lanes = BACKWARD[chunk]
    last = final and chunk == len(BACKWARD) - 1

    def before(q):
        return lane_copies(result, out, q, BACKWARD[chunk - 1], sem) if chunk > 0 else []

    def own(q):
        return lane_copies(result, out, q, lanes, sem_own) if last else []

    def launch(q, _):
        for copy in before(q):
            copy.start()
        return 0

    lax.fori_loop(0, COLS, launch, 0)

    def step(i, _):
        q = COLS - 1 - i
        backward_chain(lanes, q, source, inverse, couple, mask, result, sent)
        for copy in own(q):
            copy.start()
        if beside is not None:
            beside(jnp.maximum(q - 1, 0))
        return 0

    lax.fori_loop(0, COLS, step, 0)

    def drain(q, _):
        for copy in before(q) + own(q):
            copy.wait()
        return 0

    lax.fori_loop(0, COLS, drain, 0)


def last_kernel(chunk, inverse, rs, field, couple, mask, halo_in, halo_out, *refs):
    lanes = BACKWARD[chunk]
    source, result, out, sent, sem, sem_own = refs[-6:]
    active = lax.axis_index("strip") == STRIP - 1
    even = is_even()

    def near(q, lane):
        if 0 <= lane < LANES:
            return field[q + 1, lane]
        return halo_of(even, halo_in, halo_out, q, lane)

    def source_of(q):
        for lane in lanes:
            total = rs[q, lane] + coef(couple, 0, q, lane) * field[q, lane]
            for k, step in SIDES:
                total = total + coef(couple, k, q, lane) * near(q, lane + step)
            source[q, lane] = total

    @pl.when(active)
    def _():
        for j in range(len(lanes)):
            sent[j] = jnp.zeros((R, BS), jnp.float32)
        source_of(COLS - 1)
        backward_sweep(
            chunk, False, inverse, source, couple, mask, result, out, sent, sem, sem_own, source_of
        )

    @pl.when(jnp.logical_not(active))
    def _():
        def step(q, _):
            source_of(q)
            return 0

        lax.fori_loop(0, COLS, step, 0)


def backward_kernel(chunk, stage, came, inverse, source, couple, mask, *refs):
    result, out, sent, sem, sem_own = refs[2:]
    strip = lax.axis_index("strip")

    @pl.when(strip == stage)
    def _():
        sent[...] = came[...]
        backward_sweep(
            chunk, stage == 0, inverse, source, couple, mask, result, out, sent, sem, sem_own, None
        )

    if chunk == 0:

        @pl.when(strip == stage + 1)
        def _():
            copies = [
                pltpu.make_async_copy(
                    result.at[:, pl.ds(a, n)], out.at[:, pl.ds(a, n)], sem_own.at[i]
                )
                for i, (a, n) in enumerate(runs_of(BACKWARD[-1]))
            ]
            for copy in copies:
                copy.start()
            for copy in copies:
                copy.wait()


def vmem(shape, dtype=jnp.float32):
    return VMEM(shape, dtype)


def run(kernel, name, operands, outs, scratch, aliases=None, cost=0):
    arrays = [
        pltpu.with_memory_space_constraint(a, space) if space in (VMEM, HBM) else a
        for a, space in operands
    ]
    return pl.pallas_call(
        kernel,
        name=name,
        out_shape=[o for o, _ in outs],
        in_specs=[pl.BlockSpec(memory_space=space) for _, space in operands],
        out_specs=[pl.BlockSpec(memory_space=space) for _, space in outs],
        scratch_shapes=scratch,
        input_output_aliases=aliases or {},
        compiler_params=pltpu.CompilerParams(vmem_limit_bytes=8 * 2**20),
        cost_estimate=pl.CostEstimate(
            flops=2 ** (26 + cost), bytes_accessed=2 ** (21 + cost), transcendentals=0
        ),
    )(*arrays)


def on_device(right_side, starting_iterate, inverse_diagonal_blocks, couple, ice_mask):
    rs = right_side.reshape(FIELD)
    start = starting_iterate.reshape(FIELD)
    inverse = inverse_diagonal_blocks.reshape(BLOCKS)
    tiles = lax.axis_size("tile")
    pairs_in = [(i, i + 1) for i in range(0, tiles - 1, 2)]
    pairs_out = [(i, i + 1) for i in range(1, tiles - 1, 2)]
    to_back = [(i + 1, i) for i in range(STRIP - 1)]
    dma = pltpu.SemaphoreType.DMA

    def swapped(value, pairs):
        return lax.ppermute(value, "tile", pairs + [(b, a) for a, b in pairs])

    def inside(*arrays):
        return [(a, VMEM) for a in arrays]

    def made(*shapes):
        return [(vmem(shape), VMEM) for shape in shapes]

    def piece(lanes):
        return (len(lanes), R, BS)

    blocks = [(vmem(BLOCKS, jnp.bfloat16), VMEM)]
    inv_hbm = [(inverse, HBM)]
    now, later, edge_in, edge_out, coefs, mask, inverse = run(
        prep_kernel,
        "prep",
        [(ice_mask, HBM), (start, HBM), (couple.transpose(0, 1, 3, 2, 4), HBM)] + inv_hbm,
        made(piece(FORWARD[0]), LATER, EDGE, EDGE, COEFS, WEIGHTS) + blocks,
        [pltpu.SMEM(ice_mask.shape, jnp.int32), dma((9,)), dma((COLS,))],
    )
    now = lax.ppermute(now, "strip", to_back)
    later = lax.ppermute(later, "strip", to_back)
    halo_out = swapped(edge_out, pairs_out)
    halo_in = swapped(edge_in, pairs_in)

    sents = {}
    rest = inside(rs, start, coefs, mask)
    inverse, source, field, sent = run(
        first_kernel,
        "first",
        inv_hbm + rest + inside(inverse),
        blocks + made(FIELD, FIELD_MORE, piece(FORWARD[0])),
        [dma((COLS,))],
        {5: 0},
        cost=-10,
    )
    source, field, sents[0, 0] = run(
        tail_kernel,
        "tail",
        inside(now, inverse) + rest + inside(source, field, sent),
        made(FIELD, FIELD_MORE, piece(FORWARD[0])),
        [],
        {6: 0, 7: 1, 8: 2},
        cost=8,
    )
    inverse, source, field, sents[0, 1] = run(
        inner_kernel,
        "inner",
        inside(later) + inv_hbm + rest + inside(inverse, source, field),
        blocks + made(FIELD, FIELD_MORE, piece(FORWARD[1])),
        [dma((COLS,)), dma((COLS,))],
        {6: 0, 7: 1, 8: 2},
    )
    source, field, edge_in, edge_out, sents[0, 2] = run(
        outer_kernel,
        "outer",
        inside(now, later, halo_in, halo_out, inverse) + rest + inside(source, field),
        made(FIELD, FIELD_MORE, EDGE, EDGE, piece(FORWARD[2])),
        [],
        {9: 0, 10: 1},
    )

    for stage in range(1, STRIP):
        for chunk, lanes in enumerate(FORWARD):
            came = lax.ppermute(sents[stage - 1, chunk], "strip", [(stage - 1, stage)])
            sending = stage + 1 < STRIP
            operands = inside(came, inverse, source, coefs, mask, field)
            outs = made(FIELD_MORE)
            aliases = {5: 0}
            if chunk == OUTER:
                operands += inside(edge_in, edge_out)
                outs += made(EDGE, EDGE)
                aliases |= {6: 1, 7: 2}
            got = run(
                functools.partial(forward_kernel, chunk, stage),
                f"forward_{stage}_{chunk}",
                operands,
                outs + (made(piece(lanes)) if sending else []),
                [] if sending else [vmem(piece(lanes))],
                aliases,
            )
            field = got[0]
            if chunk == OUTER:
                edge_in, edge_out = got[1:3]
            if sending:
                sents[stage, chunk] = got[-1]

    halo_out = swapped(edge_out, pairs_out)
    halo_in = swapped(edge_in, pairs_in)

    out_shape = [(jax.ShapeDtypeStruct(FIELD, jnp.float32), HBM)]
    sems = [dma((COLS,)), dma((COLS,))]
    result = out = None
    for chunk, lanes in enumerate(BACKWARD):
        sides = inside(halo_in, halo_out) if min(lanes) < 2 or max(lanes) >= LANES - 2 else []
        operands = inside(inverse, rs, field, coefs, mask) + sides + inside(source)
        base = len(operands) - 1
        aliases = {base: 0}
        kernel = functools.partial(last_kernel, chunk)
        if not sides:
            kernel = functools.partial(without_halos, kernel)
        if chunk > 0:
            operands += inside(result) + [(out, HBM)]
            aliases |= {base + 1: 1, base + 2: 2}
        source, result, out, sents[STRIP - 1, chunk] = run(
            kernel,
            f"last_{chunk}",
            operands,
            made(FIELD, FIELD) + out_shape + made(piece(lanes)),
            sems,
            aliases,
        )

    for stage in range(STRIP - 2, -1, -1):
        for chunk, lanes in enumerate(BACKWARD):
            came = lax.ppermute(sents[stage + 1, chunk], "strip", [(stage + 1, stage)])
            sending = stage > 0
            got = run(
                functools.partial(backward_kernel, chunk, stage),
                f"backward_{stage}_{chunk}",
                inside(came, inverse, source, coefs, mask, result) + [(out, HBM)],
                made(FIELD) + out_shape + (made(piece(lanes)) if sending else []),
                ([] if sending else [vmem(piece(lanes))]) + sems,
                {5: 0, 6: 1},
            )
            result, out = got[:2]
            if sending:
                sents[stage, chunk] = got[2]
    return out.reshape(right_side.shape)


def without_halos(kernel, inverse, rs, field, couple, mask, *refs):
    kernel(inverse, rs, field, couple, mask, None, None, *refs)


def solution(mesh):
    return jax.shard_map(
        on_device,
        mesh=mesh,
        in_specs=(
            P("strip", None, "tile", None, None),
            P("strip", None, "tile", None, None),
            P("strip", None, "tile", None, None),
            P(None, "strip", None, "tile", None),
            P("strip", None, "tile"),
        ),
        out_specs=P("strip", None, "tile", None, None),
        check_vma=False,
    )
```

```python
import functools

import jax
import jax.numpy as jnp
from jax import lax
from jax.experimental import pallas as pl
from jax.experimental.pallas import tpu as pltpu
from jax.sharding import PartitionSpec as P

COLS = 8
LANES = 12
R = 32
BS = 256
FORWARD = ((2, 3, 4, 5), (0, 1, 10, 11), (6, 7, 8, 9))
BACKWARD = ((2, 3, 4, 5), (6, 7, 8, 9), (0, 1, 10, 11))
OUTER = 1
STRIP = 4
DOWN = tuple(range(COLS - 1, -1, -1))
SIDES = ((2, -1), (3, 1), (4, -2), (5, 2))
COST_TURN = 7
COST_LAST = -3
NT = (((1,), (1,)), ((), ()))
VMEM = pltpu.VMEM
ANY = pl.ANY
HBM = pltpu.HBM

FIELD = (COLS, LANES, R, BS)
FIRST = (LANES, R, BS)
FIELD_MORE = (COLS + 1, LANES, R, BS)
EDGE = (COLS, 2, R, BS)
BLOCKS = (COLS, LANES, BS, BS)
OWN_BLOCKS = (COLS, 4, BS, BS)
PER = 4
COEFS = (6, COLS // PER, LANES, PER, BS)
WEIGHTS = (COLS + 1, LANES, BS)


def runs_of(lanes):
    runs = []
    for lane in lanes:
        if runs and runs[-1][0] + runs[-1][1] == lane:
            runs[-1][1] += 1
        else:
            runs.append([lane, 1])
    return [tuple(run) for run in runs]


def coef(ref, k, q, lane):
    return ref[k, q // PER, lane, pl.ds(q % PER, 1), :]


def weight(ref, q, lane):
    return ref[q, pl.ds(lane, 1), :]


def solve(xs, inverse, q, lanes):
    alone = inverse.shape[1] < LANES
    return [
        lax.dot_general(
            x.astype(jnp.bfloat16),
            inverse[q, j if alone else lane],
            NT,
            preferred_element_type=jnp.float32,
        )
        for j, (x, lane) in enumerate(zip(xs, lanes))
    ]


def lane_copies(src, dst, q, lanes, sem):
    return [
        pltpu.make_async_copy(src.at[q, pl.ds(a, n)], dst.at[q, pl.ds(a, n)], sem.at[q])
        for a, n in runs_of(lanes)
    ]


def is_even():
    return lax.axis_index("tile") % 2 == 0


def ice_copy(ice_hbm, ice, sem):
    return pltpu.make_async_copy(ice_hbm, ice, sem)


def ice_weight(ice, q, lane):
    return ice[q // PER, q % PER, lane].astype(jnp.float32)


def prep_kernel(
    ice_hbm, st_hbm, couple_hbm, inv_hbm, nxt, edge_in, edge_out, couple, mask, own, ice, sem
):
    even = is_even()
    lane_in = jnp.where(even, LANES - 2, 0)
    lane_out = jnp.where(even, 0, LANES - 2)
    a, n = runs_of(FORWARD[0])[0]
    copies = [
        pltpu.make_async_copy(ice_hbm, ice, sem.at[0]),
        pltpu.make_async_copy(couple_hbm, couple, sem.at[1]),
        pltpu.make_async_copy(st_hbm.at[0], nxt, sem.at[2]),
        pltpu.make_async_copy(st_hbm.at[:, pl.ds(lane_out, 2)], edge_out, sem.at[3]),
        pltpu.make_async_copy(st_hbm.at[:, pl.ds(lane_in, 2)], edge_in, sem.at[4]),
        pltpu.make_async_copy(inv_hbm.at[:, pl.ds(a, n)], own, sem.at[5]),
    ]
    for copy in copies:
        copy.start()

    def ice_weight(q, lane):
        return ice[q // PER, q % PER, lane].astype(jnp.float32)

    copies[0].wait()
    for q in range(COLS):
        for lane in range(LANES):
            mask[q, pl.ds(lane, 1), :] = jnp.full((1, BS), ice_weight(q, lane), jnp.float32)
    for copy in copies[1:5]:
        copy.wait()
    for lane in range(LANES):
        nxt[lane] = weight(mask, 0, lane) * nxt[lane]
    for q in range(COLS):
        for j in range(2):
            edge_out[q, j] = ice_weight(q, lane_out + j) * edge_out[q, j]
            edge_in[q, j] = ice_weight(q, lane_in + j) * edge_in[q, j]
    copies[5].wait()


def halo_of(even, halo_in, halo_out, q, lane):
    if lane < 0:
        return jnp.where(even, halo_out[q, lane + 2], halo_in[q, lane + 2])
    return jnp.where(even, halo_in[q, lane - LANES], halo_out[q, lane - LANES])


def make_source(lanes, q, rs, start, couple, mask, source, halo=None, nxt=None):
    for lane in lanes:
        total = rs[q, lane]
        for k, step in SIDES:
            other = lane + step
            if 0 <= other < LANES:
                factor = coef(couple, k, q, lane) * weight(mask, q, other)
                total = total + factor * start[q, other]
            elif halo is not None:
                total = total + coef(couple, k, q, lane) * halo(q, other)
        if nxt is None:
            factor = coef(couple, 1, q, lane) * weight(mask, q + 1, lane)
            total = total + factor * start[q + 1, lane]
        else:
            total = total + coef(couple, 1, q, lane) * nxt[lane]
        source[q, lane] = total


def forward_chain(lanes, q, source, inverse, couple, mask, field, sent, edges=None):
    xs = [source[q, lane] + coef(couple, 0, q, lane) * sent[j] for j, lane in enumerate(lanes)]
    ys = solve(xs, inverse, q, lanes)
    values = [weight(mask, q, lane) * y for y, lane in zip(ys, lanes)]
    for j, lane in enumerate(lanes):
        field[q + 1, lane] = values[j]
        sent[j] = values[j]
    if edges is not None:
        even, edge_in, edge_out = edges
        for j in range(2):
            edge_in[q, j] = jnp.where(even, values[2 + j], values[j])
            edge_out[q, j] = jnp.where(even, values[j], values[2 + j])


def start_all(copies):
    def step(q, _):
        for copy in copies(q):
            copy.start()
        return 0

    lax.fori_loop(0, COLS, step, 0)


def wait_all(copies):
    def step(q, _):
        for copy in copies(q):
            copy.wait()
        return 0

    lax.fori_loop(0, COLS, step, 0)


def sweep_first(
    lanes, rs, start, source, inverse, couple, mask, field, sent, halo, edges, arriving=None
):
    for j in range(len(lanes)):
        sent[j] = jnp.zeros((R, BS), jnp.float32)
    make_source(lanes, 0, rs, start, couple, mask, source, halo)
    for q in range(COLS - 1):
        if arriving is not None:
            arriving(q).wait()
        forward_chain(lanes, q, source, inverse, couple, mask, field, sent, edges)
        if q + 2 < COLS:
            make_source(lanes, q + 1, rs, start, couple, mask, source, halo)


def first_kernel(
    own, inv_hbm, rs, start, couple, mask, source, field, sent, sent_last, own_last, own_outer, sem, sem_outer
):
    first = lax.axis_index("strip") == 0
    a, n = runs_of(FORWARD[2])[0]

    @pl.when(first)
    def _():
        def arriving(q):
            return pltpu.make_async_copy(inv_hbm.at[q, pl.ds(a, n)], own_last.at[q], sem.at[q])

        for q in range(COLS):
            arriving(q).start()
        outer = [
            pltpu.make_async_copy(
                inv_hbm.at[:, pl.ds(b, 2)], own_outer.at[:, pl.ds(2 * i, 2)], sem_outer.at[i]
            )
            for i, (b, _) in enumerate(runs_of(FORWARD[OUTER]))
        ]
        for copy in outer:
            copy.start()
        field[0] = jnp.zeros((LANES, R, BS), jnp.float32)
        sweep_first(
            FORWARD[0], rs, start, source, own, couple, mask, field, sent, None, None
        )
        sweep_first(
            FORWARD[2], rs, start, source, own_last, couple, mask, field, sent_last, None, None, arriving
        )
        arriving(COLS - 1).wait()
        for copy in outer:
            copy.wait()

    @pl.when(jnp.logical_not(first))
    def _():
        def step(q, _):
            make_source(range(LANES), q, rs, start, couple, mask, source)
            return 0

        lax.fori_loop(0, COLS - 1, step, 0)


def tail_kernel(chunk, nxt, own, rs, start, couple, mask, *refs):
    source, field, sent = refs[3:]
    lanes, q = FORWARD[chunk], COLS - 1
    first = lax.axis_index("strip") == 0

    @pl.when(first)
    def _():
        make_source(lanes, q, rs, start, couple, mask, source, None, nxt)
        forward_chain(lanes, q, source, own, couple, mask, field, sent)

    if chunk == 0:

        @pl.when(jnp.logical_not(first))
        def _():
            make_source(range(LANES), q, rs, start, couple, mask, source, None, nxt)


def outer_kernel(nxt, halo_in, halo_out, own, rs, start, couple, mask, *refs):
    source, field, edge_in, edge_out, sent = refs[2:]
    lanes, q = FORWARD[OUTER], COLS - 1
    even = is_even()
    edges = (even, edge_in, edge_out)
    halo = functools.partial(halo_of, even, halo_in, halo_out)

    @pl.when(lax.axis_index("strip") == 0)
    def _():
        sweep_first(lanes, rs, start, source, own, couple, mask, field, sent, halo, edges)
        make_source(lanes, q, rs, start, couple, mask, source, halo, nxt)
        forward_chain(lanes, q, source, own, couple, mask, field, sent, edges)


def halo_kernel(halo_in, halo_out, couple, _, source):
    halo = functools.partial(halo_of, is_even(), halo_in, halo_out)

    @pl.when(lax.axis_index("strip") != 0)
    def _():
        def step(q, _):
            for lane in FORWARD[OUTER]:
                total = source[q, lane]
                for k, move in SIDES:
                    if not 0 <= lane + move < LANES:
                        total = total + coef(couple, k, q, lane) * halo(q, lane + move)
                source[q, lane] = total
            return 0

        lax.fori_loop(0, COLS, step, 0)


def forward_kernel(chunk, stage, came, inverse, source, couple, mask, *refs):
    lanes = FORWARD[chunk]
    edges = None
    if chunk == OUTER:
        field, edge_in, edge_out, sent = refs[3:]
        edges = (is_even(), edge_in, edge_out)
    else:
        field, sent = refs[1:]

    @pl.when(lax.axis_index("strip") == stage)
    def _():
        for j, lane in enumerate(lanes):
            sent[j] = came[j]
            field[0, lane] = came[j]

        for q in range(COLS):
            forward_chain(lanes, q, source, inverse, couple, mask, field, sent, edges)


def backward_chain(lanes, q, source, inverse, couple, mask, result, sent):
    xs = [source[q, lane] + coef(couple, 1, q, lane) * sent[j] for j, lane in enumerate(lanes)]
    ys = solve(xs, inverse, q, lanes)
    for j, lane in enumerate(lanes):
        value = weight(mask, q, lane) * ys[j]
        result[q, lane] = value
        sent[j] = value


def backward_sweep(
    chunk, final, inverse, source, couple, mask, result, out, sent, sem, sem_own, beside
):
    lanes = BACKWARD[chunk]
    last = final and chunk == len(BACKWARD) - 1

    def before(q):
        return lane_copies(result, out, q, BACKWARD[chunk - 1], sem) if chunk > 0 else []

    def own(q):
        return lane_copies(result, out, q, lanes, sem_own) if last else []

    start_all(before)
    for q in DOWN:
        backward_chain(lanes, q, source, inverse, couple, mask, result, sent)
        for copy in own(q):
            copy.start()
        if beside is not None and q > 0:
            beside(q - 1)
    wait_all(before)
    if last:
        wait_all(own)


def last_kernel(chunk, inverse, rs, field, couple, mask, halo_in, halo_out, *refs):
    lanes = BACKWARD[chunk]
    source, result, out, sent, sem, sem_own = refs[-6:]
    active = lax.axis_index("strip") == STRIP - 1
    even = is_even()

    def near(q, lane):
        if 0 <= lane < LANES:
            return field[q + 1, lane]
        return halo_of(even, halo_in, halo_out, q, lane)

    def source_of(q):
        for lane in lanes:
            total = rs[q, lane] + coef(couple, 0, q, lane) * field[q, lane]
            for k, step in SIDES:
                total = total + coef(couple, k, q, lane) * near(q, lane + step)
            source[q, lane] = total

    @pl.when(active)
    def _():
        for j in range(len(lanes)):
            sent[j] = jnp.zeros((R, BS), jnp.float32)
        source_of(COLS - 1)
        backward_sweep(
            chunk, False, inverse, source, couple, mask, result, out, sent, sem, sem_own, source_of
        )

    @pl.when(jnp.logical_not(active))
    def _():
        def step(q, _):
            source_of(q)
            return 0

        lax.fori_loop(0, COLS, step, 0)


def backward_kernel(chunk, stage, came, inverse, source, couple, mask, *refs):
    result, out, sent, sem, sem_own = refs[2:]
    strip = lax.axis_index("strip")

    @pl.when(strip == stage)
    def _():
        sent[...] = came[...]
        backward_sweep(
            chunk, stage == 0, inverse, source, couple, mask, result, out, sent, sem, sem_own, None
        )

    if chunk == 0:

        @pl.when(strip == stage + 1)
        def _():
            copies = [
                pltpu.make_async_copy(
                    result.at[:, pl.ds(a, n)], out.at[:, pl.ds(a, n)], sem_own.at[i]
                )
                for i, (a, n) in enumerate(runs_of(BACKWARD[-1]))
            ]
            for copy in copies:
                copy.start()
            for copy in copies:
                copy.wait()


def vmem(shape, dtype=jnp.float32):
    return VMEM(shape, dtype)


def run(kernel, name, operands, outs, scratch, aliases=None, cost=0):
    arrays = [
        pltpu.with_memory_space_constraint(a, space) if space in (VMEM, HBM) else a
        for a, space in operands
    ]
    return pl.pallas_call(
        kernel,
        name=name,
        out_shape=[o for o, _ in outs],
        in_specs=[pl.BlockSpec(memory_space=space) for _, space in operands],
        out_specs=[pl.BlockSpec(memory_space=space) for _, space in outs],
        scratch_shapes=scratch,
        input_output_aliases=aliases or {},
        compiler_params=pltpu.CompilerParams(vmem_limit_bytes=8 * 2**20),
        cost_estimate=pl.CostEstimate(
            flops=2 ** (26 + cost), bytes_accessed=2 ** (21 + cost), transcendentals=0
        ),
    )(*arrays)


def on_device(right_side, starting_iterate, inverse_diagonal_blocks, couple, ice_mask):
    rs = right_side.reshape(FIELD)
    start = starting_iterate.reshape(FIELD)
    inverse = inverse_diagonal_blocks.reshape(BLOCKS)
    tiles = lax.axis_size("tile")
    pairs_in = [(i, i + 1) for i in range(0, tiles - 1, 2)]
    pairs_out = [(i, i + 1) for i in range(1, tiles - 1, 2)]
    to_back = [(i + 1, i) for i in range(STRIP - 1)]
    dma = pltpu.SemaphoreType.DMA

    def swapped(value, pairs):
        return lax.ppermute(value, "tile", pairs + [(b, a) for a, b in pairs])

    def inside(*arrays):
        return [(a, VMEM) for a in arrays]

    def made(*shapes):
        return [(vmem(shape), VMEM) for shape in shapes]

    def piece(lanes):
        return (len(lanes), R, BS)

    own_blocks = [(vmem(OWN_BLOCKS, jnp.bfloat16), VMEM)]
    nxt, edge_in, edge_out, coefs, mask, own = run(
        prep_kernel,
        "prep",
        [(ice_mask, HBM), (start, HBM), (couple.transpose(0, 1, 3, 2, 4), HBM), (inverse, HBM)],
        made(FIRST, EDGE, EDGE, COEFS, WEIGHTS) + own_blocks,
        [pltpu.SMEM(ice_mask.shape, jnp.int32), dma((6,))],
    )
    nxt = lax.ppermute(nxt, "strip", to_back)
    halo_out = swapped(edge_out, pairs_out)
    halo_in = swapped(edge_in, pairs_in)

    sents = {}
    rest = inside(rs, start, coefs, mask)
    ends = [piece(FORWARD[0]), piece(FORWARD[2])]
    source, field, sent, sent_last, own_last, own_outer = run(
        first_kernel,
        "first",
        inside(own) + [(inverse, HBM)] + rest,
        made(FIELD, FIELD_MORE, *ends) + own_blocks * 2,
        [dma((COLS,)), dma((2,))],
        cost=-10,
    )
    source, field, sents[0, 0] = run(
        functools.partial(tail_kernel, 0),
        "tail_0",
        inside(nxt, own) + rest + inside(source, field, sent),
        made(FIELD, FIELD_MORE, ends[0]),
        [],
        {6: 0, 7: 1, 8: 2},
        cost=8,
    )
    source, field, edge_in, edge_out, sents[0, 1] = run(
        outer_kernel,
        "outer",
        inside(nxt, halo_in, halo_out, own_outer) + rest + inside(source, field),
        made(FIELD, FIELD_MORE, EDGE, EDGE, piece(FORWARD[OUTER])),
        [],
        {8: 0, 9: 1},
    )
    source, field, sents[0, 2] = run(
        functools.partial(tail_kernel, 2),
        "tail_2",
        inside(nxt, own_last) + rest + inside(source, field, sent_last),
        made(FIELD, FIELD_MORE, ends[1]),
        [],
        {6: 0, 7: 1, 8: 2},
    )
    (source,) = run(
        halo_kernel, "halo", inside(halo_in, halo_out, coefs, source), made(FIELD), [], {3: 0}
    )

    for stage in range(1, STRIP):
        for chunk, lanes in enumerate(FORWARD):
            came = lax.ppermute(sents[stage - 1, chunk], "strip", [(stage - 1, stage)])
            sending = stage + 1 < STRIP
            operands = inside(came, inverse, source, coefs, mask, field)
            outs = made(FIELD_MORE)
            aliases = {5: 0}
            if chunk == OUTER:
                operands += inside(edge_in, edge_out)
                outs += made(EDGE, EDGE)
                aliases |= {6: 1, 7: 2}
            got = run(
                functools.partial(forward_kernel, chunk, stage),
                f"forward_{stage}_{chunk}",
                operands,
                outs + (made(piece(lanes)) if sending else []),
                [] if sending else [vmem(piece(lanes))],
                aliases,
                cost=COST_TURN if not sending and chunk > OUTER else 0,
            )
            field = got[0]
            if chunk == OUTER:
                edge_in, edge_out = got[1:3]
            if sending:
                sents[stage, chunk] = got[-1]

    halo_out = swapped(edge_out, pairs_out)
    halo_in = swapped(edge_in, pairs_in)

    out_shape = [(jax.ShapeDtypeStruct(FIELD, jnp.float32), HBM)]
    sems = [dma((COLS,)), dma((COLS,))]
    result = out = None
    for chunk, lanes in enumerate(BACKWARD):
        sides = inside(halo_in, halo_out) if chunk == len(BACKWARD) - 1 else []
        operands = inside(inverse, rs, field, coefs, mask) + sides + inside(source)
        base = len(operands) - 1
        aliases = {base: 0}
        kernel = functools.partial(last_kernel, chunk)
        if not sides:
            kernel = functools.partial(without_halos, kernel)
        if chunk > 0:
            operands += inside(result) + [(out, HBM)]
            aliases |= {base + 1: 1, base + 2: 2}
        source, result, out, sents[STRIP - 1, chunk] = run(
            kernel,
            f"last_{chunk}",
            operands,
            made(FIELD, FIELD) + out_shape + made(piece(lanes)),
            sems,
            aliases,
            cost=COST_LAST,
        )

    for stage in range(STRIP - 2, -1, -1):
        for chunk, lanes in enumerate(BACKWARD):
            came = lax.ppermute(sents[stage + 1, chunk], "strip", [(stage + 1, stage)])
            sending = stage > 0
            got = run(
                functools.partial(backward_kernel, chunk, stage),
                f"backward_{stage}_{chunk}",
                inside(came, inverse, source, coefs, mask, result) + [(out, HBM)],
                made(FIELD) + out_shape + (made(piece(lanes)) if sending else []),
                ([] if sending else [vmem(piece(lanes))]) + sems,
                {5: 0, 6: 1},
            )
            result, out = got[:2]
            if sending:
                sents[stage, chunk] = got[2]
    return out.reshape(right_side.shape)


def without_halos(kernel, inverse, rs, field, couple, mask, *refs):
    kernel(inverse, rs, field, couple, mask, None, None, *refs)


def solution(mesh):
    return jax.shard_map(
        on_device,
        mesh=mesh,
        in_specs=(
            P("strip", None, "tile", None, None),
            P("strip", None, "tile", None, None),
            P("strip", None, "tile", None, None),
            P(None, "strip", None, "tile", None),
            P("strip", None, "tile"),
        ),
        out_specs=P("strip", None, "tile", None, None),
        check_vma=False,
    )
```

```python
import functools

import jax
import jax.numpy as jnp
from jax import lax
from jax.experimental import pallas as pl
from jax.experimental.pallas import tpu as pltpu
from jax.sharding import PartitionSpec as P

COLS = 8
LANES = 12
R = 32
BS = 256
FORWARD = ((2, 3, 4, 5), (0, 1, 10, 11), (6, 7, 8, 9))
LEFT, RIGHT = (0, 1), (10, 11)
NEAR, FAR = 2, 3
OUTER = 1
STRIP = 4
DOWN = tuple(range(COLS - 1, -1, -1))
SIDES = ((2, -1), (3, 1), (4, -2), (5, 2))
COST_TURN = 7
COST_LAST = (-3, -3, -3, -3)
COST_BACK = (0, 0, 0, 3)
NT = (((1,), (1,)), ((), ()))
VMEM = pltpu.VMEM
ANY = pl.ANY
HBM = pltpu.HBM

FIELD = (COLS, LANES, R, BS)
FIRST = (LANES, R, BS)
FIELD_MORE = (COLS + 1, LANES, R, BS)
EDGE = (COLS, 2, R, BS)
BLOCKS = (COLS, LANES, BS, BS)
PER = 4
COEFS = (6, COLS // PER, LANES, PER, BS)
WEIGHTS = (COLS + 1, LANES, BS)


def runs_of(lanes):
    runs = []
    for lane in lanes:
        if runs and runs[-1][0] + runs[-1][1] == lane:
            runs[-1][1] += 1
        else:
            runs.append([lane, 1])
    return [tuple(run) for run in runs]


def coef(ref, k, q, lane):
    return ref[k, q // PER, lane, pl.ds(q % PER, 1), :]


def weight(ref, q, lane):
    return ref[q, pl.ds(lane, 1), :]


def solve(xs, inverse, q, lanes):
    return [
        lax.dot_general(
            x.astype(jnp.bfloat16), inverse[q, lane], NT, preferred_element_type=jnp.float32
        )
        for x, lane in zip(xs, lanes)
    ]


def lane_copies(src, dst, q, lanes, sem):
    return [
        pltpu.make_async_copy(src.at[q, pl.ds(a, n)], dst.at[q, pl.ds(a, n)], sem.at[q])
        for a, n in runs_of(lanes)
    ]


def is_even():
    return lax.axis_index("tile") % 2 == 0


def ice_copy(ice_hbm, ice, sem):
    return pltpu.make_async_copy(ice_hbm, ice, sem)


def ice_weight(ice, q, lane):
    return ice[q // PER, q % PER, lane].astype(jnp.float32)


def prep_kernel(ice_hbm, st_hbm, nxt, edge_in, edge_out, mask, ice, sem):
    even = is_even()
    lane_in = jnp.where(even, LANES - 2, 0)
    lane_out = jnp.where(even, 0, LANES - 2)
    copies = [
        pltpu.make_async_copy(ice_hbm, ice, sem.at[0]),
        pltpu.make_async_copy(st_hbm.at[0], nxt, sem.at[1]),
        pltpu.make_async_copy(st_hbm.at[:, pl.ds(lane_out, 2)], edge_out, sem.at[2]),
        pltpu.make_async_copy(st_hbm.at[:, pl.ds(lane_in, 2)], edge_in, sem.at[3]),
    ]
    for copy in copies:
        copy.start()

    def ice_weight(q, lane):
        return ice[q // PER, q % PER, lane].astype(jnp.float32)

    copies[0].wait()
    for q in range(COLS):
        for lane in range(LANES):
            mask[q, pl.ds(lane, 1), :] = jnp.full((1, BS), ice_weight(q, lane), jnp.float32)
    for copy in copies[1:]:
        copy.wait()
    for lane in range(LANES):
        nxt[lane] = weight(mask, 0, lane) * nxt[lane]
    for q in range(COLS):
        for j in range(2):
            edge_out[q, j] = ice_weight(q, lane_out + j) * edge_out[q, j]
            edge_in[q, j] = ice_weight(q, lane_in + j) * edge_in[q, j]


def halo_of(even, halo_in, halo_out, q, lane):
    if lane < 0:
        return jnp.where(even, halo_out[q, lane + 2], halo_in[q, lane + 2])
    return jnp.where(even, halo_in[q, lane - LANES], halo_out[q, lane - LANES])


def make_source(lanes, q, rs, start, couple, mask, source, halo=None, nxt=None):
    for lane in lanes:
        total = rs[q, lane]
        for k, step in SIDES:
            other = lane + step
            if 0 <= other < LANES:
                factor = coef(couple, k, q, lane) * weight(mask, q, other)
                total = total + factor * start[q, other]
            elif halo is not None:
                total = total + coef(couple, k, q, lane) * halo(q, other)
        if nxt is None:
            factor = coef(couple, 1, q, lane) * weight(mask, q + 1, lane)
            total = total + factor * start[q + 1, lane]
        else:
            total = total + coef(couple, 1, q, lane) * nxt[lane]
        source[q, lane] = total


def forward_chain(lanes, q, source, inverse, couple, mask, field, sent, edges=None):
    xs = [source[q, lane] + coef(couple, 0, q, lane) * sent[j] for j, lane in enumerate(lanes)]
    ys = solve(xs, inverse, q, lanes)
    values = [weight(mask, q, lane) * y for y, lane in zip(ys, lanes)]
    for j, lane in enumerate(lanes):
        field[q + 1, lane] = values[j]
        sent[j] = values[j]
    if edges is not None:
        even, edge_in, edge_out = edges
        for j in range(2):
            edge_in[q, j] = jnp.where(even, values[2 + j], values[j])
            edge_out[q, j] = jnp.where(even, values[j], values[2 + j])


def start_all(copies):
    def step(q, _):
        for copy in copies(q):
            copy.start()
        return 0

    lax.fori_loop(0, COLS, step, 0)


def wait_all(copies):
    def step(q, _):
        for copy in copies(q):
            copy.wait()
        return 0

    lax.fori_loop(0, COLS, step, 0)


def sweep_first(
    lanes, rs, start, source, inverse, couple, mask, field, sent, halo, edges, arriving=None
):
    for j in range(len(lanes)):
        sent[j] = jnp.zeros((R, BS), jnp.float32)
    make_source(lanes, 0, rs, start, couple, mask, source, halo)
    for q in range(COLS - 1):
        if arriving is not None:
            for copy in arriving(q):
                copy.wait()
        forward_chain(lanes, q, source, inverse, couple, mask, field, sent, edges)
        if q + 2 < COLS:
            make_source(lanes, q + 1, rs, start, couple, mask, source, halo)


def first_kernel(
    inv_hbm, couple_hbm, rs, start, mask, inverse, couple, source, field, sent, sent_last, sems, sem
):
    first = lax.axis_index("strip") == 0
    couplings = pltpu.make_async_copy(couple_hbm, couple, sem.at[0])

    def coming(lanes, at):
        return lambda q: lane_copies(inv_hbm, inverse, q, lanes, sems.at[at])

    @pl.when(first)
    def _():
        parts = [coming(FORWARD[chunk], chunk) for chunk in (0, 2, OUTER)]
        couplings.start()
        for part in parts:
            start_all(part)
        field[0] = jnp.zeros((LANES, R, BS), jnp.float32)
        couplings.wait()
        sweep_first(
            FORWARD[0], rs, start, source, inverse, couple, mask, field, sent, None, None, parts[0]
        )
        sweep_first(
            FORWARD[2], rs, start, source, inverse, couple, mask, field, sent_last, None, None, parts[1]
        )
        for copy in parts[0](COLS - 1) + parts[1](COLS - 1):
            copy.wait()
        wait_all(parts[2])

    @pl.when(jnp.logical_not(first))
    def _():
        every = coming(range(LANES), 0)
        couplings.start()
        start_all(every)
        couplings.wait()

        def step(q, _):
            make_source(range(LANES), q, rs, start, couple, mask, source)
            return 0

        lax.fori_loop(0, COLS - 1, step, 0)
        wait_all(every)


def tail_kernel(chunk, nxt, own, rs, start, couple, mask, *refs):
    source, field, sent = refs[3:]
    lanes, q = FORWARD[chunk], COLS - 1
    first = lax.axis_index("strip") == 0

    @pl.when(first)
    def _():
        make_source(lanes, q, rs, start, couple, mask, source, None, nxt)
        forward_chain(lanes, q, source, own, couple, mask, field, sent)

    if chunk == 0:

        @pl.when(jnp.logical_not(first))
        def _():
            make_source(range(LANES), q, rs, start, couple, mask, source, None, nxt)


def outer_kernel(nxt, halo_in, halo_out, own, rs, start, couple, mask, *refs):
    source, field, edge_in, edge_out, sent = refs[2:]
    lanes, q = FORWARD[OUTER], COLS - 1
    even = is_even()
    edges = (even, edge_in, edge_out)
    halo = functools.partial(halo_of, even, halo_in, halo_out)

    @pl.when(lax.axis_index("strip") == 0)
    def _():
        sweep_first(lanes, rs, start, source, own, couple, mask, field, sent, halo, edges)
        make_source(lanes, q, rs, start, couple, mask, source, halo, nxt)
        forward_chain(lanes, q, source, own, couple, mask, field, sent, edges)


def halo_kernel(halo_in, halo_out, couple, _, source):
    halo = functools.partial(halo_of, is_even(), halo_in, halo_out)

    @pl.when(lax.axis_index("strip") != 0)
    def _():
        def step(q, _):
            for lane in FORWARD[OUTER]:
                total = source[q, lane]
                for k, move in SIDES:
                    if not 0 <= lane + move < LANES:
                        total = total + coef(couple, k, q, lane) * halo(q, lane + move)
                source[q, lane] = total
            return 0

        lax.fori_loop(0, COLS, step, 0)


def forward_kernel(chunk, stage, came, inverse, source, couple, mask, *refs):
    lanes = FORWARD[chunk]
    edges = None
    if chunk == OUTER:
        field, edge_in, edge_out, sent = refs[3:]
        edges = (is_even(), edge_in, edge_out)
    else:
        field, sent = refs[1:]

    @pl.when(lax.axis_index("strip") == stage)
    def _():
        for j, lane in enumerate(lanes):
            sent[j] = came[j]
            field[0, lane] = came[j]

        for q in range(COLS):
            forward_chain(lanes, q, source, inverse, couple, mask, field, sent, edges)


def backward_chain(lanes, q, source, inverse, couple, mask, result, sent):
    xs = [source[q, lane] + coef(couple, 1, q, lane) * sent[j] for j, lane in enumerate(lanes)]
    ys = solve(xs, inverse, q, lanes)
    for j, lane in enumerate(lanes):
        value = weight(mask, q, lane) * ys[j]
        result[q, lane] = value
        sent[j] = value


def by_parity(active, even, chunk, body):
    chunks = {
        True: FORWARD[::2] + (RIGHT, LEFT),
        False: FORWARD[::2] + (LEFT, RIGHT),
    }
    if chunk < NEAR:

        @pl.when(active)
        def _():
            body(chunks[True][chunk], chunks[True][chunk - 1])

    else:

        @pl.when(jnp.logical_and(active, even))
        def _():
            body(chunks[True][chunk], chunks[True][chunk - 1])

        @pl.when(jnp.logical_and(active, jnp.logical_not(even)))
        def _():
            body(chunks[False][chunk], chunks[False][chunk - 1])


def backward_sweep(
    lanes, before, last, inverse, source, couple, mask, result, out, sent, sem, sem_own, beside
):
    def earlier(q):
        return lane_copies(result, out, q, before, sem)

    def own(q):
        return lane_copies(result, out, q, lanes, sem_own) if last else []

    if before:
        start_all(earlier)
    for q in DOWN:
        backward_chain(lanes, q, source, inverse, couple, mask, result, sent)
        for copy in own(q):
            copy.start()
        if beside is not None and q > 0:
            beside(q - 1)
    if before:
        wait_all(earlier)
    if last:
        wait_all(own)


def last_kernel(chunk, inverse, rs, field, couple, mask, halo, *refs):
    source, result, out, sent, sem, sem_own = refs[-6:]
    active = lax.axis_index("strip") == STRIP - 1
    even = is_even()

    def near(q, lane):
        if 0 <= lane < LANES:
            return field[q + 1, lane]
        return halo[q, lane + 2 if lane < 0 else lane - LANES]

    def source_of(lanes, q):
        for lane in lanes:
            total = rs[q, lane] + coef(couple, 0, q, lane) * field[q, lane]
            for k, step in SIDES:
                total = total + coef(couple, k, q, lane) * near(q, lane + step)
            source[q, lane] = total

    def sweep(lanes, before):
        for j in range(len(lanes)):
            sent[j] = jnp.zeros((R, BS), jnp.float32)
        source_of(lanes, COLS - 1)
        backward_sweep(
            lanes,
            before if chunk > 0 else None,
            False,
            inverse,
            source,
            couple,
            mask,
            result,
            out,
            sent,
            sem,
            sem_own,
            functools.partial(source_of, lanes),
        )

    def prepare(lanes, _):
        def step(q, _):
            source_of(lanes, q)
            return 0

        lax.fori_loop(0, COLS, step, 0)

    by_parity(active, even, chunk, sweep)
    by_parity(jnp.logical_not(active), even, chunk, prepare)


def backward_kernel(chunk, stage, came, inverse, source, couple, mask, *refs):
    result, out, sent, sem, sem_own = refs[2:]
    strip = lax.axis_index("strip")
    even = is_even()

    def sweep(lanes, before):
        sent[...] = came[...]
        backward_sweep(
            lanes,
            before if chunk > 0 else None,
            stage == 0 and chunk == FAR,
            inverse,
            source,
            couple,
            mask,
            result,
            out,
            sent,
            sem,
            sem_own,
            None,
        )

    def flush(lanes, _):
        copy = pltpu.make_async_copy(
            result.at[:, pl.ds(lanes[0], 2)], out.at[:, pl.ds(lanes[0], 2)], sem_own.at[0]
        )
        copy.start()
        copy.wait()

    by_parity(strip == stage, even, chunk, sweep)
    if chunk == 0:
        by_parity(strip == stage + 1, even, FAR, flush)


def vmem(shape, dtype=jnp.float32):
    return VMEM(shape, dtype)


def run(kernel, name, operands, outs, scratch, aliases=None, cost=0):
    arrays = [
        pltpu.with_memory_space_constraint(a, space) if space in (VMEM, HBM) else a
        for a, space in operands
    ]
    return pl.pallas_call(
        kernel,
        name=name,
        out_shape=[o for o, _ in outs],
        in_specs=[pl.BlockSpec(memory_space=space) for _, space in operands],
        out_specs=[pl.BlockSpec(memory_space=space) for _, space in outs],
        scratch_shapes=scratch,
        input_output_aliases=aliases or {},
        compiler_params=pltpu.CompilerParams(vmem_limit_bytes=8 * 2**20),
        cost_estimate=pl.CostEstimate(
            flops=2 ** (26 + cost), bytes_accessed=2 ** (21 + cost), transcendentals=0
        ),
    )(*arrays)


def on_device(right_side, starting_iterate, inverse_diagonal_blocks, couple, ice_mask):
    rs = right_side.reshape(FIELD)
    start = starting_iterate.reshape(FIELD)
    inverse = inverse_diagonal_blocks.reshape(BLOCKS)
    tiles = lax.axis_size("tile")
    pairs_in = [(i, i + 1) for i in range(0, tiles - 1, 2)]
    pairs_out = [(i, i + 1) for i in range(1, tiles - 1, 2)]
    to_back = [(i + 1, i) for i in range(STRIP - 1)]
    dma = pltpu.SemaphoreType.DMA

    def swapped(value, pairs):
        return lax.ppermute(value, "tile", pairs + [(b, a) for a, b in pairs])

    def inside(*arrays):
        return [(a, VMEM) for a in arrays]

    def made(*shapes):
        return [(vmem(shape), VMEM) for shape in shapes]

    def piece(lanes):
        return (len(lanes), R, BS)

    nxt, edge_in, edge_out, mask = run(
        prep_kernel,
        "prep",
        [(ice_mask, HBM), (start, HBM)],
        made(FIRST, EDGE, EDGE, WEIGHTS),
        [pltpu.SMEM(ice_mask.shape, jnp.int32), dma((4,))],
        cost=6,
    )
    nxt = lax.ppermute(nxt, "strip", to_back)
    halo_out = swapped(edge_out, pairs_out)
    halo_in = swapped(edge_in, pairs_in)

    sents = {}
    ends = [piece(FORWARD[0]), piece(FORWARD[2])]
    inverse, coefs, source, field, sent, sent_last = run(
        first_kernel,
        "first",
        [(inverse, HBM), (couple.transpose(0, 1, 3, 2, 4), HBM)] + inside(rs, start, mask),
        [(vmem(BLOCKS, jnp.bfloat16), VMEM)] + made(COEFS, FIELD, FIELD_MORE, *ends),
        [dma((3, COLS)), dma((1,))],
        cost=-10,
    )
    rest = inside(rs, start, coefs, mask)
    source, field, sents[0, 0] = run(
        functools.partial(tail_kernel, 0),
        "tail_0",
        inside(nxt, inverse) + rest + inside(source, field, sent),
        made(FIELD, FIELD_MORE, ends[0]),
        [],
        {6: 0, 7: 1, 8: 2},
        cost=8,
    )
    source, field, edge_in, edge_out, sents[0, 1] = run(
        outer_kernel,
        "outer",
        inside(nxt, halo_in, halo_out, inverse) + rest + inside(source, field),
        made(FIELD, FIELD_MORE, EDGE, EDGE, piece(FORWARD[OUTER])),
        [],
        {8: 0, 9: 1},
    )
    source, field, sents[0, 2] = run(
        functools.partial(tail_kernel, 2),
        "tail_2",
        inside(nxt, inverse) + rest + inside(source, field, sent_last),
        made(FIELD, FIELD_MORE, ends[1]),
        [],
        {6: 0, 7: 1, 8: 2},
    )
    (source,) = run(
        halo_kernel, "halo", inside(halo_in, halo_out, coefs, source), made(FIELD), [], {3: 0}
    )

    for stage in range(1, STRIP):
        for chunk, lanes in enumerate(FORWARD):
            came = lax.ppermute(sents[stage - 1, chunk], "strip", [(stage - 1, stage)])
            sending = stage + 1 < STRIP
            operands = inside(came, inverse, source, coefs, mask, field)
            outs = made(FIELD_MORE)
            aliases = {5: 0}
            if chunk == OUTER:
                operands += inside(edge_in, edge_out)
                outs += made(EDGE, EDGE)
                aliases |= {6: 1, 7: 2}
            got = run(
                functools.partial(forward_kernel, chunk, stage),
                f"forward_{stage}_{chunk}",
                operands,
                outs + (made(piece(lanes)) if sending else []),
                [] if sending else [vmem(piece(lanes))],
                aliases,
                cost=COST_TURN if not sending and chunk > OUTER else 0,
            )
            field = got[0]
            if chunk == OUTER:
                edge_in, edge_out = got[1:3]
            if sending:
                sents[stage, chunk] = got[-1]

    halo_out = swapped(edge_out, pairs_out)
    halo_in = swapped(edge_in, pairs_in)

    out_shape = [(jax.ShapeDtypeStruct(FIELD, jnp.float32), HBM)]
    sems = [dma((COLS,)), dma((COLS,))]
    result = out = None
    pieces = [piece(FORWARD[0]), piece(FORWARD[2]), piece(LEFT), piece(RIGHT)]
    for chunk, shape in enumerate(pieces):
        operands = inside(inverse, rs, field, coefs, mask)
        kernel = functools.partial(last_kernel, chunk)
        if chunk < NEAR:
            kernel = functools.partial(without_halo, kernel)
        else:
            operands += inside(halo_in if chunk == NEAR else halo_out)
        base = len(operands)
        operands += inside(source)
        aliases = {base: 0}
        if chunk > 0:
            operands += inside(result) + [(out, HBM)]
            aliases |= {base + 1: 1, base + 2: 2}
        source, result, out, sents[STRIP - 1, chunk] = run(
            kernel,
            f"last_{chunk}",
            operands,
            made(FIELD, FIELD) + out_shape + made(shape),
            sems,
            aliases,
            cost=COST_LAST[chunk],
        )

    for stage in range(STRIP - 2, -1, -1):
        for chunk, shape in enumerate(pieces):
            came = lax.ppermute(sents[stage + 1, chunk], "strip", [(stage + 1, stage)])
            sending = stage > 0
            got = run(
                functools.partial(backward_kernel, chunk, stage),
                f"backward_{stage}_{chunk}",
                inside(came, inverse, source, coefs, mask, result) + [(out, HBM)],
                made(FIELD) + out_shape + (made(shape) if sending else []),
                ([] if sending else [vmem(shape)]) + sems,
                {5: 0, 6: 1},
                cost=COST_BACK[chunk],
            )
            result, out = got[:2]
            if sending:
                sents[stage, chunk] = got[2]
    return out.reshape(right_side.shape)


def without_halo(kernel, inverse, rs, field, couple, mask, *refs):
    kernel(inverse, rs, field, couple, mask, None, *refs)


def solution(mesh):
    return jax.shard_map(
        on_device,
        mesh=mesh,
        in_specs=(
            P("strip", None, "tile", None, None),
            P("strip", None, "tile", None, None),
            P("strip", None, "tile", None, None),
            P(None, "strip", None, "tile", None),
            P("strip", None, "tile"),
        ),
        out_specs=P("strip", None, "tile", None, None),
        check_vma=False,
    )
```

```python
import functools

import jax
import jax.numpy as jnp
from jax import lax
from jax.experimental import pallas as pl
from jax.experimental.pallas import tpu as pltpu
from jax.sharding import PartitionSpec as P

COLS = 8
LANES = 12
R = 32
BS = 256
FORWARD = ((2, 3, 4, 5), (0, 1, 10, 11), (6, 7, 8, 9))
LEFT, RIGHT = (0, 1), (10, 11)
NEAR, FAR = 2, 3
OUTER = 1
STRIP = 4
DOWN = tuple(range(COLS - 1, -1, -1))
SIDES = ((2, -1), (3, 1), (4, -2), (5, 2))
COST_TURN = 7
COST_LAST = (-3, -3, -3, -3)
COST_BACK = (0, 0, 0, 3)
NT = (((1,), (1,)), ((), ()))
VMEM = pltpu.VMEM
ANY = pl.ANY
HBM = pltpu.HBM

FIELD = (COLS, LANES, R, BS)
FIRST = (LANES, R, BS)
FIELD_MORE = (COLS + 1, LANES, R, BS)
EDGE = (COLS, 2, R, BS)
BLOCKS = (COLS, LANES, BS, BS)
PER = 4
COEFS = (6, COLS // PER, LANES, PER, BS)
WEIGHTS = (COLS + 1, LANES, BS)


def runs_of(lanes):
    runs = []
    for lane in lanes:
        if runs and runs[-1][0] + runs[-1][1] == lane:
            runs[-1][1] += 1
        else:
            runs.append([lane, 1])
    return [tuple(run) for run in runs]


def coef(ref, k, q, lane):
    return ref[k, q // PER, lane, pl.ds(q % PER, 1), :]


def weight(ref, q, lane):
    return ref[q, pl.ds(lane, 1), :]


def solve(xs, inverse, q, lanes):
    return [
        lax.dot_general(
            x.astype(jnp.bfloat16), inverse[q, lane], NT, preferred_element_type=jnp.float32
        )
        for x, lane in zip(xs, lanes)
    ]


def lane_copies(src, dst, q, lanes, sem):
    return [
        pltpu.make_async_copy(src.at[q, pl.ds(a, n)], dst.at[q, pl.ds(a, n)], sem.at[q])
        for a, n in runs_of(lanes)
    ]


def is_even():
    return lax.axis_index("tile") % 2 == 0


def ice_copy(ice_hbm, ice, sem):
    return pltpu.make_async_copy(ice_hbm, ice, sem)


def ice_weight(ice, q, lane):
    return ice[q // PER, q % PER, lane].astype(jnp.float32)


def prep_kernel(ice_hbm, st_hbm, nxt, edge_in, edge_out, mask, ice, sem):
    even = is_even()
    lane_in = jnp.where(even, LANES - 2, 0)
    lane_out = jnp.where(even, 0, LANES - 2)
    copies = [
        pltpu.make_async_copy(ice_hbm, ice, sem.at[0]),
        pltpu.make_async_copy(st_hbm.at[0], nxt, sem.at[1]),
        pltpu.make_async_copy(st_hbm.at[:, pl.ds(lane_out, 2)], edge_out, sem.at[2]),
        pltpu.make_async_copy(st_hbm.at[:, pl.ds(lane_in, 2)], edge_in, sem.at[3]),
    ]
    for copy in copies:
        copy.start()

    def ice_weight(q, lane):
        return ice[q // PER, q % PER, lane].astype(jnp.float32)

    copies[0].wait()
    for q in range(COLS):
        for lane in range(LANES):
            mask[q, pl.ds(lane, 1), :] = jnp.full((1, BS), ice_weight(q, lane), jnp.float32)
    for copy in copies[1:]:
        copy.wait()
    for lane in range(LANES):
        nxt[lane] = weight(mask, 0, lane) * nxt[lane]
    for q in range(COLS):
        for j in range(2):
            edge_out[q, j] = ice_weight(q, lane_out + j) * edge_out[q, j]
            edge_in[q, j] = ice_weight(q, lane_in + j) * edge_in[q, j]


def halo_of(even, halo_in, halo_out, q, lane):
    if lane < 0:
        return jnp.where(even, halo_out[q, lane + 2], halo_in[q, lane + 2])
    return jnp.where(even, halo_in[q, lane - LANES], halo_out[q, lane - LANES])


def make_source(lanes, q, rs, start, couple, mask, source, halo=None, nxt=None):
    for lane in lanes:
        total = rs[q, lane]
        for k, step in SIDES:
            other = lane + step
            if 0 <= other < LANES:
                factor = coef(couple, k, q, lane) * weight(mask, q, other)
                total = total + factor * start[q, other]
            elif halo is not None:
                total = total + coef(couple, k, q, lane) * halo(q, other)
        if nxt is None:
            factor = coef(couple, 1, q, lane) * weight(mask, q + 1, lane)
            total = total + factor * start[q + 1, lane]
        else:
            total = total + coef(couple, 1, q, lane) * nxt[lane]
        source[q, lane] = total


def forward_chain(lanes, q, source, inverse, couple, mask, field, sent, edges=None):
    xs = [source[q, lane] + coef(couple, 0, q, lane) * sent[j] for j, lane in enumerate(lanes)]
    ys = solve(xs, inverse, q, lanes)
    values = [weight(mask, q, lane) * y for y, lane in zip(ys, lanes)]
    for j, lane in enumerate(lanes):
        field[q + 1, lane] = values[j]
        sent[j] = values[j]
    if edges is not None:
        even, edge_in, edge_out = edges
        for j in range(2):
            edge_in[q, j] = jnp.where(even, values[2 + j], values[j])
            edge_out[q, j] = jnp.where(even, values[j], values[2 + j])


def start_all(copies):
    def step(q, _):
        for copy in copies(q):
            copy.start()
        return 0

    lax.fori_loop(0, COLS, step, 0)


def wait_all(copies):
    def step(q, _):
        for copy in copies(q):
            copy.wait()
        return 0

    lax.fori_loop(0, COLS, step, 0)


def sweep_first(
    lanes, rs, start, source, inverse, couple, mask, field, sent, halo, edges, arriving=None
):
    for j in range(len(lanes)):
        sent[j] = jnp.zeros((R, BS), jnp.float32)
    make_source(lanes, 0, rs, start, couple, mask, source, halo)
    for q in range(COLS - 1):
        if arriving is not None:
            for copy in arriving(q):
                copy.wait()
        forward_chain(lanes, q, source, inverse, couple, mask, field, sent, edges)
        if q + 2 < COLS:
            make_source(lanes, q + 1, rs, start, couple, mask, source, halo)


def first_kernel(
    inv_hbm, couple_hbm, rs, start, mask, inverse, couple, source, field, sent, sent_last, sems, sem
):
    first = lax.axis_index("strip") == 0
    couplings = pltpu.make_async_copy(couple_hbm, couple, sem.at[0])

    def coming(lanes, at):
        return lambda q: lane_copies(inv_hbm, inverse, q, lanes, sems.at[at])

    @pl.when(first)
    def _():
        parts = [coming(FORWARD[chunk], chunk) for chunk in (0, 2, OUTER)]
        couplings.start()
        for part in parts:
            start_all(part)
        field[0] = jnp.zeros((LANES, R, BS), jnp.float32)
        couplings.wait()
        sweep_first(
            FORWARD[0], rs, start, source, inverse, couple, mask, field, sent, None, None, parts[0]
        )
        sweep_first(
            FORWARD[2], rs, start, source, inverse, couple, mask, field, sent_last, None, None, parts[1]
        )
        for copy in parts[0](COLS - 1) + parts[1](COLS - 1):
            copy.wait()
        wait_all(parts[2])

    @pl.when(jnp.logical_not(first))
    def _():
        every = coming(range(LANES), 0)
        couplings.start()
        start_all(every)
        couplings.wait()

        def step(q, _):
            make_source(range(LANES), q, rs, start, couple, mask, source)
            return 0

        lax.fori_loop(0, COLS - 1, step, 0)
        wait_all(every)


def tail_kernel(chunk, nxt, own, rs, start, couple, mask, *refs):
    source, field, sent = refs[3:]
    lanes, q = FORWARD[chunk], COLS - 1
    first = lax.axis_index("strip") == 0

    @pl.when(first)
    def _():
        make_source(lanes, q, rs, start, couple, mask, source, None, nxt)
        forward_chain(lanes, q, source, own, couple, mask, field, sent)

    if chunk == 0:

        @pl.when(jnp.logical_not(first))
        def _():
            make_source(range(LANES), q, rs, start, couple, mask, source, None, nxt)


def outer_kernel(nxt, halo_in, halo_out, own, rs, start, couple, mask, *refs):
    source, field, edge_in, edge_out, sent = refs[2:]
    lanes, q = FORWARD[OUTER], COLS - 1
    even = is_even()
    edges = (even, edge_in, edge_out)
    halo = functools.partial(halo_of, even, halo_in, halo_out)

    @pl.when(lax.axis_index("strip") == 0)
    def _():
        sweep_first(lanes, rs, start, source, own, couple, mask, field, sent, halo, edges)
        make_source(lanes, q, rs, start, couple, mask, source, halo, nxt)
        forward_chain(lanes, q, source, own, couple, mask, field, sent, edges)


def halo_kernel(halo_in, halo_out, couple, _, source):
    halo = functools.partial(halo_of, is_even(), halo_in, halo_out)

    @pl.when(lax.axis_index("strip") != 0)
    def _():
        def step(q, _):
            for lane in FORWARD[OUTER]:
                total = source[q, lane]
                for k, move in SIDES:
                    if not 0 <= lane + move < LANES:
                        total = total + coef(couple, k, q, lane) * halo(q, lane + move)
                source[q, lane] = total
            return 0

        lax.fori_loop(0, COLS, step, 0)


def forward_kernel(chunk, stage, came, inverse, source, couple, mask, *refs):
    lanes = FORWARD[chunk]
    edges = None
    if chunk == OUTER:
        field, edge_in, edge_out, sent = refs[3:]
        edges = (is_even(), edge_in, edge_out)
    else:
        field, sent = refs[1:]

    @pl.when(lax.axis_index("strip") == stage)
    def _():
        for j, lane in enumerate(lanes):
            sent[j] = came[j]
            field[0, lane] = came[j]

        for q in range(COLS):
            forward_chain(lanes, q, source, inverse, couple, mask, field, sent, edges)


def backward_chain(lanes, q, source, inverse, couple, mask, result, sent):
    xs = [source[q, lane] + coef(couple, 1, q, lane) * sent[j] for j, lane in enumerate(lanes)]
    ys = solve(xs, inverse, q, lanes)
    for j, lane in enumerate(lanes):
        value = weight(mask, q, lane) * ys[j]
        result[q, lane] = value
        sent[j] = value


def by_parity(active, even, chunk, body):
    chunks = {
        True: FORWARD[::2] + (RIGHT, LEFT),
        False: FORWARD[::2] + (LEFT, RIGHT),
    }
    if chunk < NEAR:

        @pl.when(active)
        def _():
            body(chunks[True][chunk], chunks[True][chunk - 1])

    else:

        @pl.when(jnp.logical_and(active, even))
        def _():
            body(chunks[True][chunk], chunks[True][chunk - 1])

        @pl.when(jnp.logical_and(active, jnp.logical_not(even)))
        def _():
            body(chunks[False][chunk], chunks[False][chunk - 1])


def backward_sweep(
    lanes, before, last, inverse, source, couple, mask, result, out, sent, sem, sem_own, beside
):
    def earlier(q):
        return lane_copies(result, out, q, before, sem)

    def own(q):
        return lane_copies(result, out, q, lanes, sem_own) if last else []

    if before:
        start_all(earlier)
    for q in DOWN:
        backward_chain(lanes, q, source, inverse, couple, mask, result, sent)
        for copy in own(q):
            copy.start()
        if beside is not None and q > 0:
            beside(q - 1)
    if before:
        wait_all(earlier)
    if last:
        wait_all(own)


def last_kernel(chunk, inverse, rs, field, couple, mask, halo, *refs):
    source, result, out, sent, sem, sem_own = refs[-6:]
    active = lax.axis_index("strip") == STRIP - 1
    even = is_even()

    def near(q, lane):
        if 0 <= lane < LANES:
            return field[q + 1, lane]
        return halo[q, lane + 2 if lane < 0 else lane - LANES]

    def source_of(lanes, q):
        for lane in lanes:
            total = rs[q, lane] + coef(couple, 0, q, lane) * field[q, lane]
            for k, step in SIDES:
                total = total + coef(couple, k, q, lane) * near(q, lane + step)
            source[q, lane] = total

    def sweep(lanes, _):
        for j in range(len(lanes)):
            sent[j] = jnp.zeros((R, BS), jnp.float32)
        source_of(lanes, COLS - 1)
        backward_sweep(
            lanes,
            None,
            False,
            inverse,
            source,
            couple,
            mask,
            result,
            out,
            sent,
            sem,
            sem_own,
            functools.partial(source_of, lanes),
        )

    def prepare(lanes, _):
        def step(q, _):
            source_of(lanes, q)
            return 0

        lax.fori_loop(0, COLS, step, 0)

    by_parity(active, even, chunk, sweep)
    by_parity(jnp.logical_not(active), even, chunk, prepare)


def backward_kernel(chunk, stage, came, inverse, source, couple, mask, *refs):
    result, out, sent, sem, sem_own = refs[2:]
    strip = lax.axis_index("strip")
    even = is_even()

    def sweep(lanes, before):
        sent[...] = came[...]
        backward_sweep(
            lanes,
            before if chunk > 0 and stage == 0 else None,
            stage == 0 and chunk == FAR,
            inverse,
            source,
            couple,
            mask,
            result,
            out,
            sent,
            sem,
            sem_own,
            None,
        )

    by_parity(strip == stage, even, chunk, sweep)
    if chunk == 0:

        @pl.when(strip == stage + 1)
        def _():
            copy = pltpu.make_async_copy(result, out, sem_own.at[0])
            copy.start()
            copy.wait()


def vmem(shape, dtype=jnp.float32):
    return VMEM(shape, dtype)


def run(kernel, name, operands, outs, scratch, aliases=None, cost=0):
    arrays = [
        pltpu.with_memory_space_constraint(a, space) if space in (VMEM, HBM) else a
        for a, space in operands
    ]
    return pl.pallas_call(
        kernel,
        name=name,
        out_shape=[o for o, _ in outs],
        in_specs=[pl.BlockSpec(memory_space=space) for _, space in operands],
        out_specs=[pl.BlockSpec(memory_space=space) for _, space in outs],
        scratch_shapes=scratch,
        input_output_aliases=aliases or {},
        compiler_params=pltpu.CompilerParams(vmem_limit_bytes=8 * 2**20),
        cost_estimate=pl.CostEstimate(
            flops=2 ** (26 + cost), bytes_accessed=2 ** (21 + cost), transcendentals=0
        ),
    )(*arrays)


def on_device(right_side, starting_iterate, inverse_diagonal_blocks, couple, ice_mask):
    rs = right_side.reshape(FIELD)
    start = starting_iterate.reshape(FIELD)
    inverse = inverse_diagonal_blocks.reshape(BLOCKS)
    tiles = lax.axis_size("tile")
    pairs_in = [(i, i + 1) for i in range(0, tiles - 1, 2)]
    pairs_out = [(i, i + 1) for i in range(1, tiles - 1, 2)]
    to_back = [(i + 1, i) for i in range(STRIP - 1)]
    dma = pltpu.SemaphoreType.DMA

    def swapped(value, pairs):
        return lax.ppermute(value, "tile", pairs + [(b, a) for a, b in pairs])

    def inside(*arrays):
        return [(a, VMEM) for a in arrays]

    def made(*shapes):
        return [(vmem(shape), VMEM) for shape in shapes]

    def piece(lanes):
        return (len(lanes), R, BS)

    nxt, edge_in, edge_out, mask = run(
        prep_kernel,
        "prep",
        [(ice_mask, HBM), (start, HBM)],
        made(FIRST, EDGE, EDGE, WEIGHTS),
        [pltpu.SMEM(ice_mask.shape, jnp.int32), dma((4,))],
        cost=6,
    )
    nxt = lax.ppermute(nxt, "strip", to_back)
    halo_out = swapped(edge_out, pairs_out)
    halo_in = swapped(edge_in, pairs_in)

    sents = {}
    ends = [piece(FORWARD[0]), piece(FORWARD[2])]
    inverse, coefs, source, field, sent, sent_last = run(
        first_kernel,
        "first",
        [(inverse, HBM), (couple.transpose(0, 1, 3, 2, 4), HBM)] + inside(rs, start, mask),
        [(vmem(BLOCKS, jnp.bfloat16), VMEM)] + made(COEFS, FIELD, FIELD_MORE, *ends),
        [dma((3, COLS)), dma((1,))],
        cost=-10,
    )
    rest = inside(rs, start, coefs, mask)
    source, field, sents[0, 0] = run(
        functools.partial(tail_kernel, 0),
        "tail_0",
        inside(nxt, inverse) + rest + inside(source, field, sent),
        made(FIELD, FIELD_MORE, ends[0]),
        [],
        {6: 0, 7: 1, 8: 2},
        cost=8,
    )
    source, field, edge_in, edge_out, sents[0, 1] = run(
        outer_kernel,
        "outer",
        inside(nxt, halo_in, halo_out, inverse) + rest + inside(source, field),
        made(FIELD, FIELD_MORE, EDGE, EDGE, piece(FORWARD[OUTER])),
        [],
        {8: 0, 9: 1},
    )
    source, field, sents[0, 2] = run(
        functools.partial(tail_kernel, 2),
        "tail_2",
        inside(nxt, inverse) + rest + inside(source, field, sent_last),
        made(FIELD, FIELD_MORE, ends[1]),
        [],
        {6: 0, 7: 1, 8: 2},
    )
    (source,) = run(
        halo_kernel, "halo", inside(halo_in, halo_out, coefs, source), made(FIELD), [], {3: 0}
    )

    for stage in range(1, STRIP):
        for chunk, lanes in enumerate(FORWARD):
            came = lax.ppermute(sents[stage - 1, chunk], "strip", [(stage - 1, stage)])
            sending = stage + 1 < STRIP
            operands = inside(came, inverse, source, coefs, mask, field)
            outs = made(FIELD_MORE)
            aliases = {5: 0}
            if chunk == OUTER:
                operands += inside(edge_in, edge_out)
                outs += made(EDGE, EDGE)
                aliases |= {6: 1, 7: 2}
            got = run(
                functools.partial(forward_kernel, chunk, stage),
                f"forward_{stage}_{chunk}",
                operands,
                outs + (made(piece(lanes)) if sending else []),
                [] if sending else [vmem(piece(lanes))],
                aliases,
                cost=COST_TURN if not sending and chunk > OUTER else 0,
            )
            field = got[0]
            if chunk == OUTER:
                edge_in, edge_out = got[1:3]
            if sending:
                sents[stage, chunk] = got[-1]

    halo_out = swapped(edge_out, pairs_out)
    halo_in = swapped(edge_in, pairs_in)

    out_shape = [(jax.ShapeDtypeStruct(FIELD, jnp.float32), HBM)]
    sems = [dma((COLS,)), dma((COLS,))]
    result = out = None
    pieces = [piece(FORWARD[0]), piece(FORWARD[2]), piece(LEFT), piece(RIGHT)]
    for chunk, shape in enumerate(pieces):
        operands = inside(inverse, rs, field, coefs, mask)
        kernel = functools.partial(last_kernel, chunk)
        if chunk < NEAR:
            kernel = functools.partial(without_halo, kernel)
        else:
            operands += inside(halo_in if chunk == NEAR else halo_out)
        base = len(operands)
        operands += inside(source)
        aliases = {base: 0}
        if chunk > 0:
            operands += inside(result) + [(out, HBM)]
            aliases |= {base + 1: 1, base + 2: 2}
        source, result, out, sents[STRIP - 1, chunk] = run(
            kernel,
            f"last_{chunk}",
            operands,
            made(FIELD, FIELD) + out_shape + made(shape),
            sems,
            aliases,
            cost=COST_LAST[chunk],
        )

    for stage in range(STRIP - 2, -1, -1):
        for chunk, shape in enumerate(pieces):
            came = lax.ppermute(sents[stage + 1, chunk], "strip", [(stage + 1, stage)])
            sending = stage > 0
            got = run(
                functools.partial(backward_kernel, chunk, stage),
                f"backward_{stage}_{chunk}",
                inside(came, inverse, source, coefs, mask, result) + [(out, HBM)],
                made(FIELD) + out_shape + (made(shape) if sending else []),
                ([] if sending else [vmem(shape)]) + sems,
                {5: 0, 6: 1},
                cost=COST_BACK[chunk],
            )
            result, out = got[:2]
            if sending:
                sents[stage, chunk] = got[2]
    return out.reshape(right_side.shape)


def without_halo(kernel, inverse, rs, field, couple, mask, *refs):
    kernel(inverse, rs, field, couple, mask, None, *refs)


def solution(mesh):
    return jax.shard_map(
        on_device,
        mesh=mesh,
        in_specs=(
            P("strip", None, "tile", None, None),
            P("strip", None, "tile", None, None),
            P("strip", None, "tile", None, None),
            P(None, "strip", None, "tile", None),
            P("strip", None, "tile"),
        ),
        out_specs=P("strip", None, "tile", None, None),
        check_vma=False,
    )
```

```python
import functools

import jax
import jax.numpy as jnp
from jax import lax
from jax.experimental import pallas as pl
from jax.experimental.pallas import tpu as pltpu
from jax.sharding import PartitionSpec as P

COLS = 8
LANES = 12
R = 32
BS = 256
FORWARD = ((2, 3, 4, 5), (0, 1, 10, 11), (6, 7, 8, 9))
LEFT, RIGHT = (0, 1), (10, 11)
NEAR, FAR = 2, 3
OUTER = 1
STRIP = 4
DOWN = tuple(range(COLS - 1, -1, -1))
SIDES = ((2, -1), (3, 1), (4, -2), (5, 2))
COST_TURN = 7
COST_LAST = (-3, -3, -3, -3)
COST_BACK = (0, 0, 0, 3)
NT = (((1,), (1,)), ((), ()))
VMEM = pltpu.VMEM
ANY = pl.ANY
HBM = pltpu.HBM

FIELD = (COLS, LANES, R, BS)
FIRST = (LANES, R, BS)
FIELD_MORE = (COLS + 1, LANES, R, BS)
EDGE = (COLS, 2, R, BS)
BLOCKS = (COLS, LANES, BS, BS)
PER = 4
COEFS = (6, COLS // PER, LANES, PER, BS)
WEIGHTS = (COLS + 1, LANES, BS)


def runs_of(lanes):
    runs = []
    for lane in lanes:
        if runs and runs[-1][0] + runs[-1][1] == lane:
            runs[-1][1] += 1
        else:
            runs.append([lane, 1])
    return [tuple(run) for run in runs]


def coef(ref, k, q, lane):
    return ref[k, q // PER, lane, pl.ds(q % PER, 1), :]


def weight(ref, q, lane):
    return ref[q, pl.ds(lane, 1), :]


def solve(xs, inverse, q, lanes):
    return [
        lax.dot_general(
            x.astype(jnp.bfloat16), inverse[q, lane], NT, preferred_element_type=jnp.float32
        )
        for x, lane in zip(xs, lanes)
    ]


def lane_copies(src, dst, q, lanes, sem):
    return [
        pltpu.make_async_copy(src.at[q, pl.ds(a, n)], dst.at[q, pl.ds(a, n)], sem.at[q])
        for a, n in runs_of(lanes)
    ]


def is_even():
    return lax.axis_index("tile") % 2 == 0


def ice_copy(ice_hbm, ice, sem):
    return pltpu.make_async_copy(ice_hbm, ice, sem)


def ice_weight(ice, q, lane):
    return ice[q // PER, q % PER, lane].astype(jnp.float32)


def prep_kernel(ice_hbm, st_hbm, nxt, edge_in, edge_out, mask, ice, sem):
    even = is_even()
    lane_in = jnp.where(even, LANES - 2, 0)
    lane_out = jnp.where(even, 0, LANES - 2)
    copies = [
        pltpu.make_async_copy(ice_hbm, ice, sem.at[0]),
        pltpu.make_async_copy(st_hbm.at[0], nxt, sem.at[1]),
        pltpu.make_async_copy(st_hbm.at[:, pl.ds(lane_out, 2)], edge_out, sem.at[2]),
        pltpu.make_async_copy(st_hbm.at[:, pl.ds(lane_in, 2)], edge_in, sem.at[3]),
    ]
    for copy in copies:
        copy.start()

    def ice_weight(q, lane):
        return ice[q // PER, q % PER, lane].astype(jnp.float32)

    copies[0].wait()
    for q in range(COLS):
        for lane in range(LANES):
            mask[q, pl.ds(lane, 1), :] = jnp.full((1, BS), ice_weight(q, lane), jnp.float32)
    for copy in copies[1:]:
        copy.wait()
    for lane in range(LANES):
        nxt[lane] = weight(mask, 0, lane) * nxt[lane]
    for q in range(COLS):
        for j in range(2):
            edge_out[q, j] = ice_weight(q, lane_out + j) * edge_out[q, j]
            edge_in[q, j] = ice_weight(q, lane_in + j) * edge_in[q, j]


def halo_of(even, halo_in, halo_out, q, lane):
    if lane < 0:
        return jnp.where(even, halo_out[q, lane + 2], halo_in[q, lane + 2])
    return jnp.where(even, halo_in[q, lane - LANES], halo_out[q, lane - LANES])


def make_source(lanes, q, rs, start, couple, mask, source, halo=None, nxt=None):
    for lane in lanes:
        total = rs[q, lane]
        for k, step in SIDES:
            other = lane + step
            if 0 <= other < LANES:
                factor = coef(couple, k, q, lane) * weight(mask, q, other)
                total = total + factor * start[q, other]
            elif halo is not None:
                total = total + coef(couple, k, q, lane) * halo(q, other)
        if nxt is None:
            factor = coef(couple, 1, q, lane) * weight(mask, q + 1, lane)
            total = total + factor * start[q + 1, lane]
        else:
            total = total + coef(couple, 1, q, lane) * nxt[lane]
        source[q, lane] = total


def forward_chain(lanes, q, source, inverse, couple, mask, field, sent, edges=None, came=None):
    prior = sent if came is None else came
    xs = [source[q, lane] + coef(couple, 0, q, lane) * prior[j] for j, lane in enumerate(lanes)]
    ys = solve(xs, inverse, q, lanes)
    values = [weight(mask, q, lane) * y for y, lane in zip(ys, lanes)]
    for j, lane in enumerate(lanes):
        field[q + 1, lane] = values[j]
        sent[j] = values[j]
    if edges is not None:
        even, edge_in, edge_out = edges
        for j in range(2):
            edge_in[q, j] = jnp.where(even, values[2 + j], values[j])
            edge_out[q, j] = jnp.where(even, values[j], values[2 + j])


def start_all(copies):
    def step(q, _):
        for copy in copies(q):
            copy.start()
        return 0

    lax.fori_loop(0, COLS, step, 0)


def wait_all(copies):
    def step(q, _):
        for copy in copies(q):
            copy.wait()
        return 0

    lax.fori_loop(0, COLS, step, 0)


def sweep_first(
    lanes, rs, start, source, inverse, couple, mask, field, sent, halo, edges, arriving=None
):
    for j in range(len(lanes)):
        sent[j] = jnp.zeros((R, BS), jnp.float32)
    make_source(lanes, 0, rs, start, couple, mask, source, halo)
    for q in range(COLS - 1):
        if arriving is not None:
            for copy in arriving(q):
                copy.wait()
        forward_chain(lanes, q, source, inverse, couple, mask, field, sent, edges)
        if q + 2 < COLS:
            make_source(lanes, q + 1, rs, start, couple, mask, source, halo)


def first_kernel(
    inv_hbm, couple_hbm, rs, start, mask, inverse, couple, source, field, sent, sent_last, sems, sem
):
    first = lax.axis_index("strip") == 0
    couplings = pltpu.make_async_copy(couple_hbm, couple, sem.at[0])

    def coming(lanes, at):
        return lambda q: lane_copies(inv_hbm, inverse, q, lanes, sems.at[at])

    @pl.when(first)
    def _():
        parts = [coming(FORWARD[chunk], chunk) for chunk in (0, 2, OUTER)]
        couplings.start()
        for part in parts:
            start_all(part)
        field[0] = jnp.zeros((LANES, R, BS), jnp.float32)
        couplings.wait()
        sweep_first(
            FORWARD[0], rs, start, source, inverse, couple, mask, field, sent, None, None, parts[0]
        )
        sweep_first(
            FORWARD[2], rs, start, source, inverse, couple, mask, field, sent_last, None, None, parts[1]
        )
        for copy in parts[0](COLS - 1) + parts[1](COLS - 1):
            copy.wait()
        wait_all(parts[2])

    @pl.when(jnp.logical_not(first))
    def _():
        every = coming(range(LANES), 0)
        couplings.start()
        start_all(every)
        couplings.wait()

        def step(q, _):
            make_source(range(LANES), q, rs, start, couple, mask, source)
            return 0

        lax.fori_loop(0, COLS - 1, step, 0)
        wait_all(every)


def tail_kernel(chunk, nxt, own, rs, start, couple, mask, *refs):
    source, field, sent = refs[3:]
    lanes, q = FORWARD[chunk], COLS - 1
    first = lax.axis_index("strip") == 0

    @pl.when(first)
    def _():
        make_source(lanes, q, rs, start, couple, mask, source, None, nxt)
        forward_chain(lanes, q, source, own, couple, mask, field, sent)

    if chunk == 0:

        @pl.when(jnp.logical_not(first))
        def _():
            make_source(range(LANES), q, rs, start, couple, mask, source, None, nxt)


def outer_kernel(nxt, halo_in, halo_out, own, rs, start, couple, mask, *refs):
    source, field, edge_in, edge_out, sent = refs[2:]
    lanes, q = FORWARD[OUTER], COLS - 1
    even = is_even()
    edges = (even, edge_in, edge_out)
    halo = functools.partial(halo_of, even, halo_in, halo_out)

    @pl.when(lax.axis_index("strip") == 0)
    def _():
        sweep_first(lanes, rs, start, source, own, couple, mask, field, sent, halo, edges)
        make_source(lanes, q, rs, start, couple, mask, source, halo, nxt)
        forward_chain(lanes, q, source, own, couple, mask, field, sent, edges)


def halo_kernel(halo_in, halo_out, couple, _, source):
    halo = functools.partial(halo_of, is_even(), halo_in, halo_out)

    @pl.when(lax.axis_index("strip") != 0)
    def _():
        def step(q, _):
            for lane in FORWARD[OUTER]:
                total = source[q, lane]
                for k, move in SIDES:
                    if not 0 <= lane + move < LANES:
                        total = total + coef(couple, k, q, lane) * halo(q, lane + move)
                source[q, lane] = total
            return 0

        lax.fori_loop(0, COLS, step, 0)


def forward_kernel(chunk, stage, came, inverse, source, couple, mask, *refs):
    lanes = FORWARD[chunk]
    edges = None
    if chunk == OUTER:
        field, edge_in, edge_out, sent = refs[3:]
        edges = (is_even(), edge_in, edge_out)
    else:
        field, sent = refs[1:]

    @pl.when(lax.axis_index("strip") == stage)
    def _():
        for j, lane in enumerate(lanes):
            field[0, lane] = came[j]

        for q in range(COLS):
            prior = came if q == 0 else None
            forward_chain(lanes, q, source, inverse, couple, mask, field, sent, edges, prior)


def backward_chain(lanes, q, source, inverse, couple, mask, result, sent, came=None):
    prior = sent if came is None else came
    xs = [source[q, lane] + coef(couple, 1, q, lane) * prior[j] for j, lane in enumerate(lanes)]
    ys = solve(xs, inverse, q, lanes)
    for j, lane in enumerate(lanes):
        value = weight(mask, q, lane) * ys[j]
        result[q, lane] = value
        sent[j] = value


def by_parity(active, even, chunk, body):
    chunks = {
        True: FORWARD[::2] + (RIGHT, LEFT),
        False: FORWARD[::2] + (LEFT, RIGHT),
    }
    if chunk < NEAR:

        @pl.when(active)
        def _():
            body(chunks[True][chunk], chunks[True][chunk - 1])

    else:

        @pl.when(jnp.logical_and(active, even))
        def _():
            body(chunks[True][chunk], chunks[True][chunk - 1])

        @pl.when(jnp.logical_and(active, jnp.logical_not(even)))
        def _():
            body(chunks[False][chunk], chunks[False][chunk - 1])


def backward_sweep(
    lanes, before, last, inverse, source, couple, mask, result, out, sent, sem, sem_own, beside, came=None
):
    def earlier(q):
        return lane_copies(result, out, q, before, sem)

    def own(q):
        return lane_copies(result, out, q, lanes, sem_own) if last else []

    if before:
        start_all(earlier)
    for q in DOWN:
        prior = came if q == DOWN[0] else None
        backward_chain(lanes, q, source, inverse, couple, mask, result, sent, prior)
        for copy in own(q):
            copy.start()
        if beside is not None and q > 0:
            beside(q - 1)
    if before:
        wait_all(earlier)
    if last:
        wait_all(own)


def last_kernel(chunk, inverse, rs, field, couple, mask, halo, *refs):
    source, result, out, sent, sem, sem_own = refs[-6:]
    active = lax.axis_index("strip") == STRIP - 1
    even = is_even()

    def near(q, lane):
        if 0 <= lane < LANES:
            return field[q + 1, lane]
        return halo[q, lane + 2 if lane < 0 else lane - LANES]

    def source_of(lanes, q):
        for lane in lanes:
            total = rs[q, lane] + coef(couple, 0, q, lane) * field[q, lane]
            for k, step in SIDES:
                total = total + coef(couple, k, q, lane) * near(q, lane + step)
            source[q, lane] = total

    def sweep(lanes, _):
        for j in range(len(lanes)):
            sent[j] = jnp.zeros((R, BS), jnp.float32)
        source_of(lanes, COLS - 1)
        backward_sweep(
            lanes,
            None,
            False,
            inverse,
            source,
            couple,
            mask,
            result,
            out,
            sent,
            sem,
            sem_own,
            functools.partial(source_of, lanes),
        )

    def prepare(lanes, _):
        def step(q, _):
            source_of(lanes, q)
            return 0

        lax.fori_loop(0, COLS, step, 0)

    by_parity(active, even, chunk, sweep)
    by_parity(jnp.logical_not(active), even, chunk, prepare)


def backward_kernel(chunk, stage, came, inverse, source, couple, mask, *refs):
    result, out, sent, sem, sem_own = refs[2:]
    strip = lax.axis_index("strip")
    even = is_even()

    def sweep(lanes, before):
        backward_sweep(
            lanes,
            before if chunk > 0 and stage == 0 else None,
            stage == 0 and chunk == FAR,
            inverse,
            source,
            couple,
            mask,
            result,
            out,
            sent,
            sem,
            sem_own,
            None,
            came,
        )

    by_parity(strip == stage, even, chunk, sweep)
    if chunk == 0:

        @pl.when(strip == stage + 1)
        def _():
            copy = pltpu.make_async_copy(result, out, sem_own.at[0])
            copy.start()
            copy.wait()


def vmem(shape, dtype=jnp.float32):
    return VMEM(shape, dtype)


def run(kernel, name, operands, outs, scratch, aliases=None, cost=0):
    arrays = [
        pltpu.with_memory_space_constraint(a, space) if space in (VMEM, HBM) else a
        for a, space in operands
    ]
    return pl.pallas_call(
        kernel,
        name=name,
        out_shape=[o for o, _ in outs],
        in_specs=[pl.BlockSpec(memory_space=space) for _, space in operands],
        out_specs=[pl.BlockSpec(memory_space=space) for _, space in outs],
        scratch_shapes=scratch,
        input_output_aliases=aliases or {},
        compiler_params=pltpu.CompilerParams(vmem_limit_bytes=8 * 2**20),
        cost_estimate=pl.CostEstimate(
            flops=2 ** (26 + cost), bytes_accessed=2 ** (21 + cost), transcendentals=0
        ),
    )(*arrays)


def on_device(right_side, starting_iterate, inverse_diagonal_blocks, couple, ice_mask):
    rs = right_side.reshape(FIELD)
    start = starting_iterate.reshape(FIELD)
    inverse = inverse_diagonal_blocks.reshape(BLOCKS)
    tiles = lax.axis_size("tile")
    pairs_in = [(i, i + 1) for i in range(0, tiles - 1, 2)]
    pairs_out = [(i, i + 1) for i in range(1, tiles - 1, 2)]
    to_back = [(i + 1, i) for i in range(STRIP - 1)]
    dma = pltpu.SemaphoreType.DMA

    def swapped(value, pairs):
        return lax.ppermute(value, "tile", pairs + [(b, a) for a, b in pairs])

    def inside(*arrays):
        return [(a, VMEM) for a in arrays]

    def made(*shapes):
        return [(vmem(shape), VMEM) for shape in shapes]

    def piece(lanes):
        return (len(lanes), R, BS)

    nxt, edge_in, edge_out, mask = run(
        prep_kernel,
        "prep",
        [(ice_mask, HBM), (start, HBM)],
        made(FIRST, EDGE, EDGE, WEIGHTS),
        [pltpu.SMEM(ice_mask.shape, jnp.int32), dma((4,))],
        cost=6,
    )
    nxt = lax.ppermute(nxt, "strip", to_back)
    halo_out = swapped(edge_out, pairs_out)
    halo_in = swapped(edge_in, pairs_in)

    sents = {}
    ends = [piece(FORWARD[0]), piece(FORWARD[2])]
    inverse, coefs, source, field, sent, sent_last = run(
        first_kernel,
        "first",
        [(inverse, HBM), (couple.transpose(0, 1, 3, 2, 4), HBM)] + inside(rs, start, mask),
        [(vmem(BLOCKS, jnp.bfloat16), VMEM)] + made(COEFS, FIELD, FIELD_MORE, *ends),
        [dma((3, COLS)), dma((1,))],
        cost=-10,
    )
    rest = inside(rs, start, coefs, mask)
    source, field, sents[0, 0] = run(
        functools.partial(tail_kernel, 0),
        "tail_0",
        inside(nxt, inverse) + rest + inside(source, field, sent),
        made(FIELD, FIELD_MORE, ends[0]),
        [],
        {6: 0, 7: 1, 8: 2},
        cost=8,
    )
    source, field, edge_in, edge_out, sents[0, 1] = run(
        outer_kernel,
        "outer",
        inside(nxt, halo_in, halo_out, inverse) + rest + inside(source, field),
        made(FIELD, FIELD_MORE, EDGE, EDGE, piece(FORWARD[OUTER])),
        [],
        {8: 0, 9: 1},
    )
    source, field, sents[0, 2] = run(
        functools.partial(tail_kernel, 2),
        "tail_2",
        inside(nxt, inverse) + rest + inside(source, field, sent_last),
        made(FIELD, FIELD_MORE, ends[1]),
        [],
        {6: 0, 7: 1, 8: 2},
    )
    (source,) = run(
        halo_kernel, "halo", inside(halo_in, halo_out, coefs, source), made(FIELD), [], {3: 0}
    )

    for stage in range(1, STRIP):
        for chunk, lanes in enumerate(FORWARD):
            came = lax.ppermute(sents[stage - 1, chunk], "strip", [(stage - 1, stage)])
            sending = stage + 1 < STRIP
            operands = inside(came, inverse, source, coefs, mask, field)
            outs = made(FIELD_MORE)
            aliases = {5: 0}
            if chunk == OUTER:
                operands += inside(edge_in, edge_out)
                outs += made(EDGE, EDGE)
                aliases |= {6: 1, 7: 2}
            got = run(
                functools.partial(forward_kernel, chunk, stage),
                f"forward_{stage}_{chunk}",
                operands,
                outs + (made(piece(lanes)) if sending else []),
                [] if sending else [vmem(piece(lanes))],
                aliases,
                cost=COST_TURN if not sending and chunk > OUTER else 0,
            )
            field = got[0]
            if chunk == OUTER:
                edge_in, edge_out = got[1:3]
            if sending:
                sents[stage, chunk] = got[-1]

    halo_out = swapped(edge_out, pairs_out)
    halo_in = swapped(edge_in, pairs_in)

    out_shape = [(jax.ShapeDtypeStruct(FIELD, jnp.float32), HBM)]
    sems = [dma((COLS,)), dma((COLS,))]
    result = out = None
    pieces = [piece(FORWARD[0]), piece(FORWARD[2]), piece(LEFT), piece(RIGHT)]
    for chunk, shape in enumerate(pieces):
        operands = inside(inverse, rs, field, coefs, mask)
        kernel = functools.partial(last_kernel, chunk)
        if chunk < NEAR:
            kernel = functools.partial(without_halo, kernel)
        else:
            operands += inside(halo_in if chunk == NEAR else halo_out)
        base = len(operands)
        operands += inside(source)
        aliases = {base: 0}
        if chunk > 0:
            operands += inside(result) + [(out, HBM)]
            aliases |= {base + 1: 1, base + 2: 2}
        source, result, out, sents[STRIP - 1, chunk] = run(
            kernel,
            f"last_{chunk}",
            operands,
            made(FIELD, FIELD) + out_shape + made(shape),
            sems,
            aliases,
            cost=COST_LAST[chunk],
        )

    for stage in range(STRIP - 2, -1, -1):
        for chunk, shape in enumerate(pieces):
            came = lax.ppermute(sents[stage + 1, chunk], "strip", [(stage + 1, stage)])
            sending = stage > 0
            got = run(
                functools.partial(backward_kernel, chunk, stage),
                f"backward_{stage}_{chunk}",
                inside(came, inverse, source, coefs, mask, result) + [(out, HBM)],
                made(FIELD) + out_shape + (made(shape) if sending else []),
                ([] if sending else [vmem(shape)]) + sems,
                {5: 0, 6: 1},
                cost=COST_BACK[chunk],
            )
            result, out = got[:2]
            if sending:
                sents[stage, chunk] = got[2]
    return out.reshape(right_side.shape)


def without_halo(kernel, inverse, rs, field, couple, mask, *refs):
    kernel(inverse, rs, field, couple, mask, None, *refs)


def solution(mesh):
    return jax.shard_map(
        on_device,
        mesh=mesh,
        in_specs=(
            P("strip", None, "tile", None, None),
            P("strip", None, "tile", None, None),
            P("strip", None, "tile", None, None),
            P(None, "strip", None, "tile", None),
            P("strip", None, "tile"),
        ),
        out_specs=P("strip", None, "tile", None, None),
        check_vma=False,
    )
```
